128 devices in a mesh: outer: 16 (over x, y), inner: 8 (over z, core).
Axes of the slice: x: 4, y: 4, z: 4, core: 2. Of those that a mesh axis runs over, the one named last changes fastest.
Arguments:
- tokens: bfloat16 [2048, 4096], P(('outer', 'inner')), may hold values from -6 to 6
- out_grad: bfloat16 [2048, 4096], P(('outer', 'inner')), may hold values from -2 to 2
- combine: float32 [2048, 4], P(('outer', 'inner')), may hold values from 0.1 to 1
- expert_ids: int32 [2048, 4], P(('outer', 'inner')), may hold values from 0 to 31, all different within a row; in each aligned block of 16 rows (0 to 15, 16 to 31, ...) at most 4 rows name the same one
- gate_weight: bfloat16 [128, 4096, 384], P(('outer', 'inner')), may hold values from -0.09375 to 0.09375
- up_weight: bfloat16 [128, 4096, 384], P(('outer', 'inner')), may hold values from -0.09375 to 0.09375
- down_weight: bfloat16 [128, 384, 4096], P(('outer', 'inner')), may hold values from -0.15625 to 0.15625
Outputs:
- token_grad: bfloat16 [2048, 4096], P(('outer', 'inner'))
- combine_grad: float32 [2048, 4], P(('outer', 'inner'))
- gate_grad: bfloat16 [128, 4096, 384], P(('outer', 'inner'))
- up_grad: bfloat16 [128, 4096, 384], P(('outer', 'inner'))
- down_grad: bfloat16 [128, 384, 4096], P(('outer', 'inner'))
The draws below stay inside these ranges and needn't reach their ends.
Inputs may be any that keep to these rules, and one draw needn't show every extreme that they name: `expert_ids`: each row names 4 different experts. In the rows of one device no expert is named by more than 4 rows, a bound that some block reaches.
All inputs are finite; a program needn't handle non-finite values.
Results may differ from the reference program's by a relative error of at most 0.018.
Values may be sent and summed in bfloat16 or wider, within the bound.
No kernel may reach another device: no remote copies, remote signals or barrier semaphores. Data moves between devices by JAX's collectives and lax.ppermute only.
A program may use at most 128 MiB of HBM per device.

```python
import math
import jax
import jax.numpy as jnp
import numpy as np
from jax import lax

D = 4096
FF = 1536
TOPK = 4
SPLIT = 4
TOK_DEV = 16
FF_DEV = 384
EXPERTS = 32
TOKENS = 2048
CAP = 4
N_OUTER = 16
N_INNER = 8


def levels(own_key, shape, split, low, largest):
    def one(position, shards_of):
        steps = jax.random.uniform(jax.random.fold_in(jax.random.fold_in(own_key, 6), position), (shards_of,), jnp.float32, low / len(split), largest / len(split))
        return jnp.repeat(jnp.exp(steps), shape[position] // shards_of).reshape((-1,) + (1,) * (len(shape) - position - 1))

    gain = one(*split[0])
    for cut in split[1:]:
        gain = gain * one(*cut)
    return gain


def deal_out(stream_key, own, number, rows, count, top, reach, skew):
    sequence = jax.random.permutation(stream_key, count)
    heavy_load, usual = shares(count, rows * top, reach, skew, True), shares(count, rows * top, reach, skew, False)
    places = jnp.arange(count)

    def named(tallies, rotation):
        used = int((tallies > 0).sum())
        fixed = max(1, used // 4)
        moved = fixed + (places - fixed + rotation * (used - fixed)) % max(1, count - fixed)
        return jnp.zeros((count,), jnp.int32).at[sequence[jnp.where(places < fixed, places, moved)]].set(jnp.asarray(tallies, jnp.int32))

    tallies = jnp.where(number % 4 == 0, named(heavy_load, number // 4), named(usual, number - number // 4 - 1))
    mixed = jax.random.permutation(jax.random.fold_in(own, 3), count)
    giver, taker = mixed[0:count // 2 * 2:2], mixed[1:count // 2 * 2:2]
    slack = jnp.minimum(tallies[giver] - 1, reach - tallies[taker]) // 2
    slack = jnp.where((giver == sequence[0]) | (taker == sequence[0]) | (tallies[taker] == 0), 0, jnp.maximum(slack, 0))
    moved = jax.random.randint(jax.random.fold_in(own, 4), (count // 2,), 0, 1 << 20) % (slack + 1)
    tallies = tallies.at[giver].add(-moved).at[taker].add(moved)
    labels = jnp.searchsorted(jnp.cumsum(tallies), jnp.arange(rows * top), side="right").astype(jnp.int32)
    grid = labels.reshape(top, rows).T
    grid = grid[jax.random.permutation(jax.random.fold_in(own, 1), rows)]
    rotation = jax.random.randint(jax.random.fold_in(own, 2), (rows, 1), 0, top)
    return jnp.take_along_axis(grid, (jnp.arange(top)[None, :] + rotation) % top, axis=1)


def shares(amount, total, limit, skew, full):
    loads = [(1 << 20) // math.isqrt(rank ** skew) + 1 for rank in range(1, amount + 1)]
    largest = limit if full else min(limit, max(-(-total // amount), total * loads[0] // sum(loads)))
    least = 1 if total - largest >= amount - 1 else 0
    holding, spare = [largest] + [least] * (amount - 1), total - largest - least * (amount - 1)
    while spare > 0:
        candidates = [i for i in range(1, amount) if holding[i] < largest] or [i for i in range(1, amount) if holding[i] < limit]
        pool, left = sum([loads[i] for i in candidates]), spare
        for i in candidates:
            addition = min(limit - holding[i], max(1, left * loads[i] // pool), spare)
            holding[i] = holding[i] + addition
            spare = spare - addition
    return np.array(holding)


def scatter_about(rng, shape, deviation, reach, shards=(), kind=jnp.bfloat16):
    array = deviation * jax.random.normal(rng, shape, jnp.float32)
    if shards:
        array = array * levels(rng, shape, shards, -0.22, 0.18)
    return jnp.clip(array, -reach, reach).astype(kind)


def setup_inputs(seed: int = 0) -> dict:
    keys = jax.random.split(jax.random.key(seed), 8)
    tokens = scatter_about(keys[0], (TOKENS, D), 1.0, 6.0, ((0, 128),))
    out_grad = scatter_about(keys[1], (TOKENS, D), 0.3, 2.0, ((0, 128),))
    combine = jnp.clip(0.1 + 0.9 * jax.random.uniform(keys[2], (TOKENS, TOPK), jnp.float32) ** levels(keys[2], (TOKENS, TOPK), ((0, 128),), -0.2, 0.2), 0.1, 1.0)
    expert_ids_keys = jax.random.split(jax.random.fold_in(keys[3], 1), TOKENS // TOK_DEV)
    expert_ids_turns = jax.random.permutation(jax.random.fold_in(keys[3], 3), TOKENS // TOK_DEV)
    expert_ids = jax.vmap(lambda own, number: deal_out(jax.random.fold_in(keys[3], 2), own, number, TOK_DEV, EXPERTS, TOPK, CAP, 2))(expert_ids_keys, expert_ids_turns).reshape((TOKENS, TOPK))
    gate_weight = scatter_about(keys[4], (EXPERTS * SPLIT, D, FF_DEV), D ** -0.5, 0.09375, ((0, 128),))
    up_weight = scatter_about(keys[5], (EXPERTS * SPLIT, D, FF_DEV), D ** -0.5, 0.09375, ((0, 128),))
    down_weight = scatter_about(keys[6], (EXPERTS * SPLIT, FF_DEV, D), FF ** -0.5, 0.15625, ((0, 128),))
    return dict(tokens=tokens, out_grad=out_grad, combine=combine, expert_ids=expert_ids, gate_weight=gate_weight, up_weight=up_weight, down_weight=down_weight)


def expert_backward(rows_in, rows_grad, row_weight, gate_w, up_w, down_w):
    gate_pre = jnp.dot(rows_in, gate_w, preferred_element_type=jnp.float32)
    up_pre = jnp.dot(rows_in, up_w, preferred_element_type=jnp.float32)
    sigmoid_gate = jax.nn.sigmoid(gate_pre)
    active = gate_pre * sigmoid_gate
    hidden = (active * up_pre).astype(jnp.bfloat16)
    cols_dims = (((1,), (1,)), ((), ()))
    rows_dims = (((0,), (0,)), ((), ()))
    back_grad = lax.dot_general(rows_grad, down_w, cols_dims, preferred_element_type=jnp.float32)
    row_score = jnp.sum(back_grad * hidden.astype(jnp.float32), axis=1)
    scaled = row_weight[:, None] * back_grad
    weighted = (row_weight[:, None] * hidden.astype(jnp.float32)).astype(jnp.bfloat16)
    d_gate = (scaled * up_pre * sigmoid_gate * (1.0 + gate_pre * (1.0 - sigmoid_gate))).astype(jnp.bfloat16)
    d_up = (scaled * active).astype(jnp.bfloat16)
    gate_grad = lax.dot_general(rows_in, d_gate, rows_dims, preferred_element_type=jnp.float32).astype(jnp.bfloat16)
    up_grad = lax.dot_general(rows_in, d_up, rows_dims, preferred_element_type=jnp.float32).astype(jnp.bfloat16)
    down_grad = lax.dot_general(weighted, rows_grad, rows_dims, preferred_element_type=jnp.float32).astype(jnp.bfloat16)
    row_part = (lax.dot_general(d_gate, gate_w, cols_dims, preferred_element_type=jnp.float32)
                + lax.dot_general(d_up, up_w, cols_dims, preferred_element_type=jnp.float32)).astype(jnp.bfloat16)
    return row_part, row_score, gate_grad, up_grad, down_grad


def reference(tokens, out_grad, combine, expert_ids, gate_weight, up_weight, down_weight):
    devices = N_OUTER * N_INNER
    pairs = TOKENS * TOPK
    grouped = expert_ids.reshape(devices, TOK_DEV * TOPK)
    onehot = (grouped[:, :, None] == jnp.arange(EXPERTS, dtype=jnp.int32)[None, None, :]).astype(jnp.int32)
    ranks = jnp.sum((jnp.cumsum(onehot, axis=1) - 1) * onehot, axis=2)
    sources = jnp.arange(devices, dtype=jnp.int32)[:, None]
    columns = (sources * CAP + ranks).reshape(-1).astype(jnp.int32)
    experts_of = grouped.reshape(-1).astype(jnp.int32)
    table = jnp.full((EXPERTS, devices * CAP), pairs, jnp.int32)
    table = table.at[experts_of, columns].set(jnp.arange(pairs, dtype=jnp.int32))
    pad_in = jnp.concatenate([tokens, jnp.zeros((1, D), tokens.dtype)], axis=0)
    pad_grad = jnp.concatenate([out_grad, jnp.zeros((1, D), out_grad.dtype)], axis=0)
    pad_weight = jnp.concatenate([combine.reshape(-1), jnp.zeros((1,), jnp.float32)], axis=0)

    def shard_step(carry, index):
        token_acc, score_acc = carry
        picks = table[index // SPLIT]
        token_rows = picks // TOPK
        row_part, row_score, gate_grad, up_grad, down_grad = expert_backward(
            pad_in[token_rows], pad_grad[token_rows], pad_weight[picks],
            gate_weight[index], up_weight[index], down_weight[index])
        token_acc = token_acc.at[token_rows].add(row_part.astype(jnp.float32))
        score_acc = score_acc.at[picks].add(row_score)
        return (token_acc, score_acc), (gate_grad, up_grad, down_grad)

    start = (jnp.zeros((TOKENS + 1, D), jnp.float32), jnp.zeros((pairs + 1,), jnp.float32))
    final, grads = lax.scan(shard_step, start, jnp.arange(EXPERTS * SPLIT, dtype=jnp.int32))
    token_grad = final[0][:TOKENS].astype(jnp.bfloat16)
    combine_grad = final[1][:pairs].reshape(TOKENS, TOPK)
    return token_grad, combine_grad, grads[0], grads[1], grads[2]
```

```python
import functools

import jax
import jax.numpy as jnp
from jax import lax
from jax.experimental import pallas as pl
from jax.experimental.pallas import tpu as pltpu
from jax.sharding import Mesh
from jax.sharding import PartitionSpec as P

SPLIT = 4
CORES = 2
SLOTS = 8
CHIPS = ("outer", "z")
ALL = ("outer", "z", "core")
SCORE = 128


def slot_mask(ids_t, first, rows):
    tok = ids_t.shape[1]
    line = lax.broadcasted_iota(jnp.int32, (rows, tok), 0) + first
    expert = line // (CORES * SLOTS)
    slot = line % SLOTS
    named = jnp.zeros((rows, tok), jnp.float32)
    for k in range(ids_t.shape[0]):
        named += jnp.where(ids_t[k : k + 1, :] == expert, 1.0, 0.0)
    before = lax.broadcasted_iota(jnp.int32, (tok, tok), 0)
    after = lax.broadcasted_iota(jnp.int32, (tok, tok), 1)
    half = tok // CORES
    earlier = jnp.where((before < after) & (before // half == after // half), 1.0, 0.0)
    rank = jnp.dot(named, earlier, preferred_element_type=jnp.float32).astype(jnp.int32)
    token = lax.broadcasted_iota(jnp.int32, (rows, tok), 1)
    place = rank + (token // half) * (SLOTS // CORES)
    return jnp.where((named > 0.0) & (place == slot), 1.0, 0.0), expert


def build_kernel(scaled, ids_ref, comb_ref, rows_ref, out_ref):
    block = out_ref.shape[0]
    ids_t = ids_ref[...]
    mask, expert = slot_mask(ids_t, pl.program_id(0) * block, block)
    picked = jnp.dot(mask.astype(jnp.bfloat16), rows_ref[...], preferred_element_type=jnp.float32)
    if scaled:
        weight = jnp.zeros_like(mask)
        for k in range(ids_t.shape[0]):
            weight += jnp.where(ids_t[k : k + 1, :] == expert, comb_ref[k : k + 1, :], 0.0)
        picked = picked * jnp.sum(weight * mask, axis=1, keepdims=True)
    out_ref[...] = picked.astype(out_ref.dtype)


def build(scaled, ids_t, comb_t, rows, lines):
    width = rows.shape[1]
    block = 128
    return pl.pallas_call(
        functools.partial(build_kernel, scaled),
        grid=(lines // block,),
        in_specs=[
            pl.BlockSpec(ids_t.shape, lambda i: (0, 0)),
            pl.BlockSpec(comb_t.shape, lambda i: (0, 0)),
            pl.BlockSpec(rows.shape, lambda i: (0, 0)),
        ],
        out_specs=pl.BlockSpec((block, width), lambda i: (i, 0)),
        out_shape=jax.ShapeDtypeStruct((lines, width), rows.dtype),
        name="build_scaled" if scaled else "build_plain",
    )(ids_t, comb_t, rows)


def combine_kernel(ids_ref, comb_ref, back_ref, out_ref, score_ref):
    lines, total = back_ref.shape
    width = total - SCORE
    ids_t = ids_ref[...]
    mask, expert = slot_mask(ids_t, 0, lines)
    out_ref[...] = lax.dot_general(
        mask.astype(jnp.bfloat16), back_ref[:, :width], (((0,), (0,)), ((), ())), preferred_element_type=jnp.float32
    ).astype(out_ref.dtype)
    score = back_ref[:, width : width + 1].astype(jnp.float32) * mask
    for k in range(ids_t.shape[0]):
        picked = jnp.sum(jnp.where(ids_t[k : k + 1, :] == expert, score, 0.0), axis=0, keepdims=True)
        score_ref[k : k + 1, :] = picked / comb_ref[k : k + 1, :]


def expert_backward(rows_in, rows_grad, gate_w, up_w, down_w):
    gate_pre = jnp.dot(rows_in, gate_w, preferred_element_type=jnp.float32)
    up_pre = jnp.dot(rows_in, up_w, preferred_element_type=jnp.float32)
    sigmoid_gate = jax.nn.sigmoid(gate_pre)
    active = gate_pre * sigmoid_gate
    hidden = (active * up_pre).astype(jnp.bfloat16)
    cols_dims = (((1,), (1,)), ((), ()))
    rows_dims = (((0,), (0,)), ((), ()))
    scaled = lax.dot_general(rows_grad, down_w, cols_dims, preferred_element_type=jnp.float32)
    row_score = jnp.sum(scaled * hidden.astype(jnp.float32), axis=1)
    d_gate = (scaled * up_pre * sigmoid_gate * (1.0 + gate_pre * (1.0 - sigmoid_gate))).astype(jnp.bfloat16)
    d_up = (scaled * active).astype(jnp.bfloat16)
    gate_grad = lax.dot_general(rows_in, d_gate, rows_dims, preferred_element_type=jnp.float32).astype(jnp.bfloat16)
    up_grad = lax.dot_general(rows_in, d_up, rows_dims, preferred_element_type=jnp.float32).astype(jnp.bfloat16)
    down_grad = lax.dot_general(hidden, rows_grad, rows_dims, preferred_element_type=jnp.float32).astype(jnp.bfloat16)
    row_part = (
        lax.dot_general(d_gate, gate_w, cols_dims, preferred_element_type=jnp.float32)
        + lax.dot_general(d_up, up_w, cols_dims, preferred_element_type=jnp.float32)
    ).astype(jnp.bfloat16)
    return row_part, row_score, gate_grad, up_grad, down_grad


def swap(x):
    return lax.ppermute(x, "core", [(0, 1), (1, 0)])


def local(tokens, out_grad, combine, expert_ids, gate_weight, up_weight, down_weight):
    chips = lax.axis_size("outer") * lax.axis_size("z")
    lines = chips * SLOTS
    tok, width = tokens.shape
    half = width // CORES
    core = lax.axis_index("core")
    first = core == 0

    def in_order(own, other, axis):
        return jnp.where(first, jnp.concatenate([own, other], axis), jnp.concatenate([other, own], axis))

    def halves(x):
        left, right = x[:, :half], x[:, half:]
        return jnp.where(first, left, right), jnp.where(first, right, left)

    ids = in_order(expert_ids, swap(expert_ids), 0).T
    comb = in_order(combine, swap(combine), 0).T
    tok_own, tok_send = halves(tokens)
    grad_own, grad_send = halves(out_grad)
    tok_half = in_order(tok_own, swap(tok_send), 0)
    grad_half = in_order(grad_own, swap(grad_send), 0)

    def deliver(x):
        return lax.all_to_all(x, CHIPS, split_axis=0, concat_axis=0, tiled=True)

    rows_own = deliver(build(False, ids, comb, tok_half, lines))
    rows_in = in_order(rows_own, swap(rows_own), 1)
    grads_own = deliver(build(True, ids, comb, grad_half, lines))
    rows_grad = in_order(grads_own, swap(grads_own), 1)

    row_part, row_score, gate_grad, up_grad, down_grad = expert_backward(
        rows_in, rows_grad, gate_weight[0], up_weight[0], down_weight[0]
    )
    part_own, part_send = halves(row_part)
    part = (part_own.astype(jnp.float32) + swap(part_send).astype(jnp.float32)).astype(jnp.bfloat16)
    score = jnp.broadcast_to(row_score.astype(jnp.bfloat16)[:, None], (lines, SCORE))
    back = deliver(jnp.concatenate([part, score], axis=1))

    token_half, score = pl.pallas_call(
        combine_kernel,
        out_shape=(
            jax.ShapeDtypeStruct((CORES * tok, half), jnp.bfloat16),
            jax.ShapeDtypeStruct(ids.shape, jnp.float32),
        ),
        name="combine_rows",
    )(ids, comb, back)
    grad_mine = jnp.where(first, token_half[:tok], token_half[tok:])
    grad_other = jnp.where(first, token_half[tok:], token_half[:tok])
    token_grad = in_order(grad_mine, swap(grad_other), 1)
    score_mine = jnp.where(first, score[:, :tok], score[:, tok:])
    score_other = jnp.where(first, score[:, tok:], score[:, :tok])
    combine_grad = (score_mine + swap(score_other)).T
    return token_grad, combine_grad, gate_grad[None], up_grad[None], down_grad[None]


def solution(mesh):
    outer, inner = mesh.devices.shape
    split = Mesh(mesh.devices.reshape(outer, inner // CORES, CORES), ALL)
    flat, deep = P(ALL, None), P(ALL, None, None)
    return jax.shard_map(
        local,
        mesh=split,
        in_specs=(flat, flat, flat, flat, deep, deep, deep),
        out_specs=(flat, flat, deep, deep, deep),
        check_vma=False,
    )
```

```python
import functools

import jax
import jax.numpy as jnp
from jax import lax
from jax.experimental import pallas as pl
from jax.experimental.pallas import tpu as pltpu
from jax.sharding import Mesh
from jax.sharding import PartitionSpec as P

CORES = 2
CAP = 4
SLOTS = CORES * CAP
META = 128
CHIPS = ("outer", "z")
ALL = ("outer", "z", "core")
F32 = jnp.float32
BF16 = jnp.bfloat16
TN = (((0,), (0,)), ((), ()))
NT = (((1,), (1,)), ((), ()))
SMEM = pl.BlockSpec(memory_space=pltpu.SMEM)
HBM = pl.BlockSpec(memory_space=pltpu.HBM)


def dot(a, b, dims=(((1,), (0,)), ((), ()))):
    return lax.dot_general(a, b, dims, preferred_element_type=F32)


def after(x, *others):
    return lax.optimization_barrier((x, *others))


class Loaded:
    def __init__(self, source, target, semaphore):
        self.copy = pltpu.make_async_copy(source, target, semaphore)
        self.target = target
        self.shape = target.shape
        self.waiting = True
        self.copy.start()

    def wait(self):
        if self.waiting:
            self.copy.wait()
            self.waiting = False

    def __getitem__(self, index):
        self.wait()
        return self.target[index]


def call(kernel, name, outs, place, *args, raw=0, direct=0, scratch=(), limit=63 << 20):
    count, given = len(outs) - direct, len(args) - raw

    def body(place_ref, *refs):
        raw_refs, ins, refs = refs[:raw], refs[raw : raw + given], refs[raw + given :]
        out_refs, direct_refs, refs = refs[:count], refs[count : count + direct], refs[count + direct :]
        held, made, refs = refs[:given], refs[given : given + count], refs[given + count :]
        in_sems, out_sems, own = refs[0], refs[1], refs[2:]
        loaded = [Loaded(ins[n], held[n], in_sems.at[n]) for n in range(given)]
        kernel(place_ref, *raw_refs, *loaded, *made, *direct_refs, *own)
        for held_ref in loaded:
            held_ref.wait()
        copies = [pltpu.make_async_copy(made[n], out_refs[n], out_sems.at[n]) for n in range(count)]
        for copy in copies:
            copy.start()
        for copy in copies:
            copy.wait()

    return pl.pallas_call(
        body,
        in_specs=[SMEM] + [HBM] * len(args),
        out_specs=[HBM] * len(outs),
        out_shape=[jax.ShapeDtypeStruct(shape, kind) for shape, kind in outs],
        scratch_shapes=[pltpu.VMEM(x.shape, x.dtype) for x in args[raw:]]
        + [pltpu.VMEM(shape, kind) for shape, kind in outs[:count]]
        + [pltpu.SemaphoreType.DMA((max(given, 1),)), pltpu.SemaphoreType.DMA((max(count, 1),)), *scratch],
        compiler_params=pltpu.CompilerParams(vmem_limit_bytes=limit),
        name=name,
    )(place, *args)


def column(row):
    n = row.shape[1]
    here = lax.broadcasted_iota(jnp.int32, (n, n), 0) == lax.broadcasted_iota(jnp.int32, (n, n), 1)
    return jnp.sum(jnp.where(here, row, 0.0), axis=1, keepdims=True)


def row(column):
    n = column.shape[0]
    here = lax.broadcasted_iota(jnp.int32, (n, n), 0) == lax.broadcasted_iota(jnp.int32, (n, n), 1)
    return jnp.sum(jnp.where(here, column, 0.0), axis=0, keepdims=True)


def columns(start, size):
    return pl.ds(pl.multiple_of(start, size), size)


def pack_kernel(place_ref, tok_ref, grad_ref, ids_ref, comb_ref, *out_refs):
    tok, width = tok_ref.shape
    me = place_ref[0]
    lane = lax.broadcasted_iota(jnp.int32, (tok, META), 1)
    ids, comb = ids_ref[...].astype(F32), comb_ref[...]
    high = comb.astype(BF16).astype(F32)
    low = comb - high
    meta = jnp.zeros((tok, META), F32)
    topk = ids.shape[0]
    for part, value in enumerate((ids, high, low)):
        for k in range(topk):
            meta = jnp.where(lane == part * topk + k, column(value[k : k + 1, :]), meta)
    meta = meta.astype(BF16)
    for j, out_ref in enumerate(out_refs):
        piece = out_ref.shape[1] - META
        which = (me % CORES) ^ j
        out_ref[:tok, :piece] = tok_ref[:, columns(which * piece, piece)]
        out_ref[tok:, :piece] = grad_ref[:, columns(which * piece, piece)]
        out_ref[:tok, piece:] = meta
        out_ref[tok:, piece:] = jnp.zeros_like(meta)


def slot_mask(core, meta, lines):
    tokens = meta.shape[0]
    own = tokens // CORES
    line = lax.broadcasted_iota(jnp.int32, (tokens, lines), 1)
    expert = (line // (2 * SLOTS)).astype(F32)
    named = [jnp.where(meta[:, k : k + 1] == expert, 1.0, 0.0) for k in range(4)]
    total = named[0] + named[1] + named[2] + named[3]
    after = lax.broadcasted_iota(jnp.int32, (tokens, tokens), 0)
    before = lax.broadcasted_iota(jnp.int32, (tokens, tokens), 1)
    earlier = jnp.where((before < after) & (before // own == after // own), 1.0, 0.0)
    rank = dot(earlier.astype(BF16), total.astype(BF16)).astype(jnp.int32)
    token = lax.broadcasted_iota(jnp.int32, (tokens, lines), 0)
    place = rank + ((token // own) ^ core) * CAP
    mask = jnp.where((total > 0.0) & (place == line % SLOTS), 1.0, 0.0)
    return mask, named


def meta_of(refs, tok):
    width = refs[0].shape[1] - META
    return jnp.concatenate([ref[:tok, width:] for ref in refs], axis=0).astype(F32)


def build_kernel(scaled, place_ref, own_ref, other_ref, out_ref):
    refs = (own_ref, other_ref)
    lines, half = out_ref.shape
    tok = own_ref.shape[0] // 2
    meta = meta_of(refs, tok)
    mask, named = slot_mask(place_ref[0], meta, lines)
    pick = mask.astype(BF16)
    if scaled:
        ones = jnp.ones((mask.shape[0], META), BF16)
        weight = jnp.zeros((lines, META), F32)
        for part in (1, 2):
            chosen = sum(named[k] * meta[:, part * 4 + k : part * 4 + k + 1] for k in range(4)) * mask
            weight += dot(chosen.astype(BF16), ones, TN)
        weight = weight[:, :1]
    first = tok if scaled else 0
    step = 512
    for at in range(0, half, step):
        found = dot(pick, jnp.concatenate([ref[first : first + tok, at : at + step] for ref in refs], axis=0), TN)
        out_ref[:, at : at + step] = (found * weight if scaled else found).astype(BF16)


def gate_up_kernel(place_ref, gate_hbm, up_hbm, own_ref, other_ref, out_ref, first_ref, sems):
    core = place_ref[0]
    half = own_ref.shape[1]
    parts, _, both = first_ref.shape
    ff, quarter = both // 2, CORES * half // parts
    copies = []
    for n in range(parts):
        at = columns(((core ^ (n * CORES // parts)) * half) + (n * quarter) % half, quarter)
        copies += [
            pltpu.make_async_copy(gate_hbm.at[0, at, :], first_ref.at[n, :, pl.ds(0, ff)], sems.at[2 * n]),
            pltpu.make_async_copy(up_hbm.at[0, at, :], first_ref.at[n, :, pl.ds(ff, ff)], sems.at[2 * n + 1]),
        ]
    for copy in copies:
        copy.start()
    pre = 0.0
    for n in range(parts):
        ref, at = (own_ref, other_ref)[n * CORES // parts], (n * quarter) % half
        rows = ref[:, at : at + quarter]
        copies[2 * n].wait()
        copies[2 * n + 1].wait()
        pre += dot(rows, first_ref[n])
    out_ref[...] = pre


def back_product(down_hbm, which, grads_ref, down_ref, sems):
    half = grads_ref.shape[1]
    step = half // CORES
    copies = []
    for n in range(CORES):
        at = columns(which * half + n * step, step)
        copies.append(pltpu.make_async_copy(down_hbm.at[0, :, at], down_ref.at[n], sems.at[n]))
    for copy in copies:
        copy.start()
    scaled = 0.0
    for n, copy in enumerate(copies):
        grads = grads_ref[:, n * step : (n + 1) * step]
        copy.wait()
        scaled += dot(grads, down_ref[n], NT)
    return scaled


def back_early_kernel(place_ref, down_hbm, own_ref, out_ref, down_ref, sems):
    out_ref[...] = back_product(down_hbm, place_ref[0], own_ref, down_ref, sems)


def back_late_kernel(place_ref, down_hbm, other_ref, sum_ref, pre_ref, deltas_ref, hidden_ref, score_ref, down_ref, sems):
    scaled = back_product(down_hbm, 1 - place_ref[0], other_ref, down_ref, sems) + sum_ref[...]
    ff = hidden_ref.shape[1]
    gate_pre, up_pre = pre_ref[:, :ff], pre_ref[:, ff:]
    sigmoid_gate = jax.nn.sigmoid(gate_pre)
    active = gate_pre * sigmoid_gate
    hidden = (active * up_pre).astype(BF16)
    score = jnp.sum(scaled * hidden.astype(F32), axis=1, keepdims=True)
    deltas_ref[:, :ff] = (scaled * up_pre * sigmoid_gate * (1.0 + gate_pre * (1.0 - sigmoid_gate))).astype(BF16)
    deltas_ref[:, ff:] = (scaled * active).astype(BF16)
    hidden_ref[...] = hidden
    score_ref[...] = jnp.broadcast_to(score, score_ref.shape).astype(BF16)


def lend_kernel(place_ref, gate_hbm, up_hbm, out_ref, sems):
    half, both = out_ref.shape
    ff = both // 2
    at = columns((1 - place_ref[0]) * half, half)
    copies = [
        pltpu.make_async_copy(gate_hbm.at[0, at, :], out_ref.at[:, pl.ds(0, ff)], sems.at[0]),
        pltpu.make_async_copy(up_hbm.at[0, at, :], out_ref.at[:, pl.ds(ff, ff)], sems.at[1]),
    ]
    for copy in copies:
        copy.start()
    for copy in copies:
        copy.wait()


def parts_kernel(place_ref, gate_hbm, up_hbm, lent_hbm, own_ref, other_ref, score_ref, out_ref, weight_ref, sems):
    steps, _, step, both = weight_ref.shape
    half, ff = steps * step, both // 2
    start = place_ref[0] * half
    copies = []
    for n in range(steps):
        at = columns(start + n * step, step)
        pairs = (
            (gate_hbm.at[0, at, :], weight_ref.at[n, 0, :, pl.ds(0, ff)]),
            (up_hbm.at[0, at, :], weight_ref.at[n, 0, :, pl.ds(ff, ff)]),
            (lent_hbm.at[pl.ds(n * step, step), :], weight_ref.at[n, 1]),
        )
        copies.append([pltpu.make_async_copy(*pair, sems.at[3 * n + k]) for k, pair in enumerate(pairs)])
    for some in copies:
        for copy in some:
            copy.start()
    out_ref[:, half:] = score_ref[...]
    own, other = own_ref[...], other_ref[...]
    for n, some in enumerate(copies):
        for copy in some:
            copy.wait()
        part = dot(own, weight_ref[n, 0], NT) + dot(other, weight_ref[n, 1], NT)
        out_ref[:, n * step : (n + 1) * step] = part.astype(BF16)


def gather_kernel(place_ref, own_ref, other_ref, back_ref, mark_ref, mine_ref, send_ref):
    lines, total = back_ref.shape
    width = total - META
    tok = own_ref.shape[0] // 2
    mask, named = slot_mask(place_ref[0], meta_of((own_ref, other_ref), tok), lines)
    pick = mask.astype(BF16)
    step = 512
    for at in range(0, width, step):
        part = dot(pick, back_ref[:, at : at + step]).astype(BF16)
        mine_ref[:, at : at + step] = part[:tok]
        send_ref[:, at : at + step] = part[tok:]
    scores = back_ref[:, width:]
    lane = lax.broadcasted_iota(jnp.int32, (mask.shape[0], META), 1)
    found = jnp.zeros((mask.shape[0], META), F32)
    for k in range(4):
        found = jnp.where(lane == k, dot((mask * named[k]).astype(BF16), scores), found)
    mine_ref[:, width:] = found[:tok].astype(BF16)
    send_ref[:, width:] = found[tok:].astype(BF16)


def final_kernel(place_ref, comb_ref, own_ref, other_ref, out_ref, score_ref):
    core = place_ref[0]
    width = own_ref.shape[1] - META
    out_ref[:, columns(core * width, width)] = own_ref[:, :width]
    out_ref[:, columns((1 - core) * width, width)] = other_ref[:, :width]
    score = own_ref[:, width:].astype(F32) + other_ref[:, width:].astype(F32)
    for k in range(comb_ref.shape[0]):
        score_ref[k : k + 1, :] = row(score[:, k : k + 1]) / comb_ref[k : k + 1, :]


def weights_kernel(place_ref, *refs):
    rows_refs, grads_refs = refs[0:2], refs[2:4]
    deltas_ref, hidden_ref, mark_ref, gate_hbm, up_hbm, down_hbm, gate_ref, up_ref, down_ref, sems = refs[4:]
    mark_ref[...] = jnp.zeros_like(mark_ref)
    core = place_ref[0]
    half, step = rows_refs[0].shape[1], gate_ref.shape[1]
    ff = hidden_ref.shape[1]
    deltas = deltas_ref[...]
    copies = []
    for j in range(CORES):
        for at in range(0, half, step):
            n = (j * half + at) // step
            grad = dot(rows_refs[j][:, at : at + step], deltas, TN)
            gate_ref[n] = grad[:, :ff].astype(BF16)
            up_ref[n] = grad[:, ff:].astype(BF16)
            cols = columns((core ^ j) * half + at, step)
            copies += [
                pltpu.make_async_copy(gate_ref.at[n], gate_hbm.at[0, cols, :], sems.at[3 * n]),
                pltpu.make_async_copy(up_ref.at[n], up_hbm.at[0, cols, :], sems.at[3 * n + 1]),
            ]
            for copy in copies[-2:]:
                copy.start()
    hidden = hidden_ref[...].T
    for j in range(CORES):
        for at in range(0, half, step):
            n = (j * half + at) // step
            down_ref[n] = dot(hidden, grads_refs[j][:, at : at + step]).astype(BF16)
            cols = columns((core ^ j) * half + at, step)
            copies.append(pltpu.make_async_copy(down_ref.at[n], down_hbm.at[0, :, cols], sems.at[3 * n + 2]))
            copies[-1].start()
    for copy in copies:
        copy.wait()


def local(tokens, out_grad, combine, expert_ids, gate_weight, up_weight, down_weight):
    tok, width = tokens.shape
    chips = lax.axis_size(CHIPS)
    lines = chips * SLOTS
    ff = gate_weight.shape[2]
    half, quarter = width // CORES, width // CORES // 2
    step = 512
    place = lax.axis_index("core").astype(jnp.int32).reshape(1)

    def swap(x):
        return lax.ppermute(x, "core", [(0, 1), (1, 0)])

    def deliver(x):
        found = lax.all_to_all(x.reshape(chips, SLOTS, x.shape[1]), CHIPS, split_axis=0, concat_axis=0, tiled=True)
        return found.reshape(x.shape)

    own, send = call(
        pack_kernel, "pack", [((2 * tok, half + META), BF16)] * CORES,
        place, tokens, out_grad, expert_ids.T, combine.T,
    )
    messages = (own, swap(send))

    def build(scaled):
        kernel = functools.partial(build_kernel, scaled)
        return call(kernel, "build", [((lines, half), BF16)], place, *messages)[0]

    rows_out = build(False)
    grads_out = build(True)
    lend = call(
        lend_kernel, "lend", [((half, 2 * ff), BF16)], place, gate_weight, up_weight,
        raw=2, scratch=[pltpu.SemaphoreType.DMA((2,))],
    )[0]
    rows, grads_out, lend = after(deliver(rows_out), grads_out, lend)
    lent = swap(lend)
    rows_pair = (rows, swap(rows))
    pre = call(
        gate_up_kernel, "gate_up", [((lines, 2 * ff), F32)], place, gate_weight, up_weight, *rows_pair,
        raw=2, scratch=[pltpu.VMEM((4, quarter, 2 * ff), BF16), pltpu.SemaphoreType.DMA((8,))],
    )[0]
    grads, pre, lent = after(deliver(grads_out), pre, lent)
    grads_pair = (grads, swap(grads))
    scratch = [pltpu.VMEM((CORES, ff, quarter), BF16), pltpu.SemaphoreType.DMA((CORES,))]
    scaled = call(
        back_early_kernel, "back_early", [((lines, ff), F32)], place, down_weight, grads_pair[0], raw=1, scratch=scratch
    )[0]
    other, scaled = after(grads_pair[1], scaled)
    deltas, hidden, score = call(
        back_late_kernel,
        "back_late",
        [((lines, 2 * ff), BF16), ((lines, ff), BF16), ((lines, META), BF16)],
        place, down_weight, other, scaled, pre, raw=1, scratch=scratch,
    )
    parts = call(
        parts_kernel,
        "row_parts",
        [((lines, half + META), BF16)],
        place, gate_weight, up_weight, lent, deltas, swap(deltas), score,
        raw=3,
        scratch=[
            pltpu.VMEM((half // step, 2, step, 2 * ff), BF16),
            pltpu.SemaphoreType.DMA((3 * half // step,)),
        ],
    )[0]
    mark, gate_grad, up_grad, down_grad = call(
        weights_kernel,
        "weight_grads",
        [((8, META), F32), (gate_weight.shape, BF16), (up_weight.shape, BF16), (down_weight.shape, BF16)],
        place, *rows_pair, *grads_pair, deltas, hidden,
        direct=3,
        scratch=[
            pltpu.VMEM((width // step, step, ff), BF16),
            pltpu.VMEM((width // step, step, ff), BF16),
            pltpu.VMEM((width // step, ff, step), BF16),
            pltpu.SemaphoreType.DMA((3 * width // step,)),
        ],
    )
    mine, send = call(
        gather_kernel, "gather_rows", [((tok, half + META), BF16)] * CORES, place, *messages, deliver(parts), mark
    )
    token_grad, combine_grad = call(
        final_kernel, "total", [(tokens.shape, BF16), (combine.shape[::-1], F32)], place, combine.T, mine, swap(send)
    )
    return token_grad, combine_grad.T, gate_grad, up_grad, down_grad


def solution(mesh):
    outer, inner = mesh.devices.shape
    split = Mesh(mesh.devices.reshape(outer, inner // CORES, CORES), ALL)
    flat, deep = P(ALL, None), P(ALL, None, None)
    return jax.shard_map(
        local,
        mesh=split,
        in_specs=(flat, flat, flat, flat, deep, deep, deep),
        out_specs=(flat, flat, deep, deep, deep),
        check_vma=False,
    )
```

```python
import functools

import jax
import jax.numpy as jnp
from jax import lax
from jax.experimental import pallas as pl
from jax.experimental.pallas import tpu as pltpu
from jax.sharding import Mesh
from jax.sharding import PartitionSpec as P

CORES = 2
TOPK = 4
CAP = 4
SLOTS = CORES * CAP
META = 128
CHIPS = ("outer", "z")
ALL = ("outer", "z", "core")
F32 = jnp.float32
BF16 = jnp.bfloat16
TN = (((0,), (0,)), ((), ()))
NT = (((1,), (1,)), ((), ()))
SMEM = pl.BlockSpec(memory_space=pltpu.SMEM)
HBM = pl.BlockSpec(memory_space=pltpu.HBM)


def dot(a, b, dims=(((1,), (0,)), ((), ()))):
    return lax.dot_general(a, b, dims, preferred_element_type=F32)


def after(x, *others):
    return lax.optimization_barrier((x, *others))


class Loaded:
    def __init__(self, source, target, semaphore):
        self.copy = pltpu.make_async_copy(source, target, semaphore)
        self.target = target
        self.shape = target.shape
        self.waiting = True
        self.copy.start()

    def wait(self):
        if self.waiting:
            self.copy.wait()
            self.waiting = False

    def __getitem__(self, index):
        self.wait()
        return self.target[index]


class Stages:
    def __init__(self, groups, depth):
        self.groups, self.depth = groups, depth
        for copy in sum(groups[:depth], []):
            copy.start()

    def wait(self, n):
        for copy in self.groups[n]:
            copy.wait()
        for copy in sum(self.groups[n + self.depth : n + self.depth + 1], []):
            copy.start()


def call(kernel, name, outs, place, *args, raw=0, direct=0, scratch=(), limit=28 << 20, far=False):
    count, given = len(outs) - direct, len(args) - raw

    def body(place_ref, *refs):
        raw_refs, ins, refs = refs[:raw], refs[raw : raw + given], refs[raw + given :]
        out_refs, direct_refs, refs = refs[:count], refs[count : count + direct], refs[count + direct :]
        held, made, refs = refs[:given], refs[given : given + count], refs[given + count :]
        in_sems, out_sems, own = refs[0], refs[1], refs[2:]
        loaded = [Loaded(ins[n], held[n], in_sems.at[n]) for n in range(given)]
        kernel(place_ref, *raw_refs, *loaded, *made, *direct_refs, *own)
        for held_ref in loaded:
            held_ref.wait()
        copies = [pltpu.make_async_copy(made[n], out_refs[n], out_sems.at[n]) for n in range(count)]
        for copy in copies:
            copy.start()
        for copy in copies:
            copy.wait()

    return pl.pallas_call(
        body,
        in_specs=[SMEM] + [HBM] * len(args),
        out_specs=[HBM] * len(outs),
        out_shape=[pltpu.HBM(*out) if far else jax.ShapeDtypeStruct(*out) for out in outs],
        scratch_shapes=[pltpu.VMEM(x.shape, x.dtype) for x in args[raw:]]
        + [pltpu.VMEM(shape, kind) for shape, kind in outs[:count]]
        + [pltpu.SemaphoreType.DMA((max(given, 1),)), pltpu.SemaphoreType.DMA((max(count, 1),)), *scratch],
        compiler_params=pltpu.CompilerParams(vmem_limit_bytes=limit),
        name=name,
    )(place, *args)


def column(row):
    n = row.shape[1]
    here = lax.broadcasted_iota(jnp.int32, (n, n), 0) == lax.broadcasted_iota(jnp.int32, (n, n), 1)
    return jnp.sum(jnp.where(here, row, 0.0), axis=1, keepdims=True)


def row(column):
    n = column.shape[0]
    here = lax.broadcasted_iota(jnp.int32, (n, n), 0) == lax.broadcasted_iota(jnp.int32, (n, n), 1)
    return jnp.sum(jnp.where(here, column, 0.0), axis=0, keepdims=True)


def columns(start, size):
    return pl.ds(pl.multiple_of(start, size), size)


def slot_mask(core, ids, lines):
    tokens = ids[0].shape[0]
    own = tokens // CORES
    line = lax.broadcasted_iota(jnp.int32, (tokens, lines), 1)
    expert = (line // (2 * SLOTS)).astype(F32)
    named = [jnp.where(some == expert, 1.0, 0.0) for some in ids]
    total = named[0] + named[1] + named[2] + named[3]
    after = lax.broadcasted_iota(jnp.int32, (tokens, tokens), 0)
    before = lax.broadcasted_iota(jnp.int32, (tokens, tokens), 1)
    earlier = jnp.where((before < after) & (before // own == after // own), 1.0, 0.0)
    rank = dot(earlier.astype(BF16), total.astype(BF16)).astype(jnp.int32)
    token = lax.broadcasted_iota(jnp.int32, (tokens, lines), 0)
    place = rank + ((token // own) ^ core) * CAP
    mask = jnp.where((total > 0.0) & (place == line % SLOTS), 1.0, 0.0)
    return mask, named


def both_of(refs, k):
    return jnp.concatenate([column(ref[k : k + 1, :].astype(F32)) for ref in refs], axis=0)


def build_kernel(place_ref, ids_ref, other_ids_ref, *refs):
    scaled = len(refs) > 5
    if scaled:
        comb_refs, rows_refs, (picks_ref, out_hbm, out_ref, sems) = refs[0:2], refs[2:4], refs[4:]
    else:
        rows_refs, (out_hbm, out_ref, sems) = refs[0:2], refs[2:]
    core = place_ref[0]
    steps, lines, step = out_ref.shape
    tok, width = rows_refs[0].shape
    half = width // CORES
    ids_refs = (ids_ref, other_ids_ref)
    mask, named = slot_mask(core, [both_of(ids_refs, k) for k in range(TOPK)], lines)
    pick = mask.astype(BF16)
    if scaled:
        picks_ref[: CORES * tok, :] = pick
        for k in range(TOPK):
            picks_ref[(k + 1) * CORES * tok : (k + 2) * CORES * tok, :] = (mask * named[k]).astype(BF16)
        chosen = sum(named[k] * both_of(comb_refs, k) for k in range(TOPK)) * mask
        high = chosen.astype(BF16)
        ones = jnp.ones((mask.shape[0], META), BF16)
        weight = dot(high, ones, TN) + dot((chosen - high.astype(F32)).astype(BF16), ones, TN)
        weight = weight[:, :1]
    copies = []
    for n in range(steps):
        cols = columns(core * half + n * step, step)
        found = dot(pick, jnp.concatenate([ref[:, cols] for ref in rows_refs], axis=0), TN)
        out_ref[n] = (found * weight if scaled else found).astype(BF16)
        copies.append(pltpu.make_async_copy(out_ref.at[n], out_hbm.at[:, pl.ds(n * step, step)], sems.at[n]))
        copies[-1].start()
    for copy in copies:
        copy.wait()


def lend_kernel(place_ref, gate_hbm, up_hbm, order_hbm, first_ref, sems):
    half, both = first_ref.shape
    ff = both // 2
    at = columns((1 - place_ref[0]) * half, half)
    copies = [
        pltpu.make_async_copy(gate_hbm.at[0, at, :], first_ref.at[:, pl.ds(0, ff)], sems.at[0]),
        pltpu.make_async_copy(up_hbm.at[0, at, :], first_ref.at[:, pl.ds(ff, ff)], sems.at[1]),
    ]
    for copy in copies:
        copy.start()
    for copy in copies:
        copy.wait()


def turn_kernel(place_ref, gate_hbm, up_hbm, down_hbm, order_hbm, back_ref, parts_ref, first_ref, down_ref, sems):
    half, both = first_ref.shape
    ff = both // 2
    at = columns(place_ref[0] * half, half)
    copies = [
        pltpu.make_async_copy(down_hbm.at[0], down_ref, sems.at[0]),
        pltpu.make_async_copy(gate_hbm.at[0, at, :], first_ref.at[:, pl.ds(0, ff)], sems.at[1]),
        pltpu.make_async_copy(up_hbm.at[0, at, :], first_ref.at[:, pl.ds(ff, ff)], sems.at[2]),
    ]
    for copy in copies:
        copy.start()
    for copy in copies:
        copy.wait()
    step = 256
    for n in range(0, CORES * half, step):
        back_ref[n : n + step, :] = down_ref[:, n : n + step].T
    for n in range(0, half, step):
        parts_ref[:, n : n + step] = first_ref[n : n + step, :].T


def turn_lent_kernel(place_ref, lent_ref, parts_ref):
    step = 256
    for n in range(0, lent_ref.shape[0], step):
        parts_ref[:, n : n + step] = lent_ref[n : n + step, :].T


def gate_up_kernel(place_ref, gate_hbm, up_hbm, own_hbm, other_hbm, factors_ref, hidden_ref, rows_ref, first_ref, sems):
    core = place_ref[0]
    parts, step, both = first_ref.shape
    ff = both // 2
    half = parts * step // CORES
    groups = []
    for n in range(parts):
        j, at = divmod(n * step, half)
        cols = columns((core ^ j) * half + at, step)
        pairs = (
            ((own_hbm, other_hbm)[j].at[:, pl.ds(at, step)], rows_ref.at[n]),
            (gate_hbm.at[0, cols, :], first_ref.at[n, :, pl.ds(0, ff)]),
            (up_hbm.at[0, cols, :], first_ref.at[n, :, pl.ds(ff, ff)]),
        )
        groups.append([pltpu.make_async_copy(*pair, sems.at[3 * n + k]) for k, pair in enumerate(pairs)])
    stages = Stages(groups, 2)
    pre = 0.0
    for n in range(parts):
        stages.wait(n)
        pre += dot(rows_ref[n], first_ref[n])
    gate_pre, up_pre = pre[:, :ff], pre[:, ff:]
    sigmoid_gate = jax.nn.sigmoid(gate_pre)
    active = gate_pre * sigmoid_gate
    hidden_ref[...] = (active * up_pre).astype(BF16)
    factors_ref[:, :ff] = up_pre * sigmoid_gate * (1.0 + gate_pre * (1.0 - sigmoid_gate))
    factors_ref[:, ff:] = active


def back_product(which, back_hbm, grads_hbm, rows_ref, back_ref, sems):
    parts, _, step = rows_ref.shape
    groups = []
    for n in range(parts):
        at = columns((which * parts + n) * step, step)
        pairs = ((grads_hbm.at[:, pl.ds(n * step, step)], rows_ref.at[n]), (back_hbm.at[at, :], back_ref.at[n]))
        groups.append([pltpu.make_async_copy(*pair, sems.at[2 * n + k]) for k, pair in enumerate(pairs)])
    stages = Stages(groups, parts)
    scaled = 0.0
    for n in range(parts):
        stages.wait(n)
        scaled += dot(rows_ref[n], back_ref[n])
    return scaled


def back_early_kernel(place_ref, back_hbm, own_hbm, out_ref, *own):
    out_ref[...] = back_product(place_ref[0], back_hbm, own_hbm, *own)


def back_late_kernel(place_ref, back_hbm, other_hbm, sum_ref, factors_ref, hidden_ref, deltas_ref, score_ref, *own):
    scaled = back_product(1 - place_ref[0], back_hbm, other_hbm, *own) + sum_ref[...]
    ff = scaled.shape[1]
    score = jnp.sum(scaled * hidden_ref[...].astype(F32), axis=1, keepdims=True)
    deltas_ref[:, :ff] = (scaled * factors_ref[:, :ff]).astype(BF16)
    deltas_ref[:, ff:] = (scaled * factors_ref[:, ff:]).astype(BF16)
    score_ref[...] = jnp.broadcast_to(score, score_ref.shape).astype(BF16)


def parts_kernel(last, place_ref, turned_hbm, deltas_ref, *refs):
    if last:
        before_ref, score_ref, *refs = refs
    out_hbm, weight_ref, part_ref, sems, out_sems = refs
    steps, _, step = weight_ref.shape
    half = steps * step
    stages = Stages([
        [pltpu.make_async_copy(turned_hbm.at[:, pl.ds(n * step, step)], weight_ref.at[n], sems.at[n])]
        for n in range(steps)
    ], 2)
    deltas = deltas_ref[...]
    outs = []
    for n in range(steps):
        stages.wait(n)
        part = dot(deltas, weight_ref[n])
        if last:
            part += before_ref[:, n * step : (n + 1) * step].astype(F32)
        part_ref[n] = part.astype(BF16)
        outs.append(pltpu.make_async_copy(part_ref.at[n], out_hbm.at[:, pl.ds(n * step, step)], out_sems.at[n]))
        outs[-1].start()
    if last:
        score_ref.wait()
        outs.append(pltpu.make_async_copy(score_ref.target, out_hbm.at[:, pl.ds(half, META)], out_sems.at[steps]))
        outs[-1].start()
    for copy in outs:
        copy.wait()


def gather_kernel(place_ref, back_hbm, picks_ref, mark_ref, mine_ref, send_ref, mine_score_ref, send_score_ref, back_ref, sems):
    tok, width = mine_ref.shape
    tokens = CORES * tok
    steps, _, step = back_ref.shape
    copies = [pltpu.make_async_copy(back_hbm.at[:, pl.ds(width, META)], back_ref.at[steps - 1, :, pl.ds(0, META)], sems.at[0])]
    for n in range(steps - 1):
        copies.append(pltpu.make_async_copy(back_hbm.at[:, pl.ds(n * step, step)], back_ref.at[n], sems.at[n + 1]))
    for copy in copies:
        copy.start()
    pick = picks_ref[:tokens, :]
    copies[0].wait()
    scores = dot(picks_ref[tokens:, :], back_ref[steps - 1, :, :META])
    for k in range(TOPK):
        mine_score_ref[k : k + 1, :] = row(scores[k * tokens : k * tokens + tok, :1])
        send_score_ref[k : k + 1, :] = row(scores[k * tokens + tok : (k + 1) * tokens, :1])
    for n in range(steps - 1):
        copies[n + 1].wait()
        part = dot(pick, back_ref[n]).astype(BF16)
        mine_ref[:, n * step : (n + 1) * step] = part[:tok]
        send_ref[:, n * step : (n + 1) * step] = part[tok:]


def weights_kernel(place_ref, *refs):
    rows_refs, grads_refs = refs[0:2], refs[2:4]
    deltas_ref, hidden_ref, mark_ref, gate_hbm, up_hbm, down_hbm, gate_ref, up_ref, down_ref, sems = refs[4:]
    mark_ref[...] = jnp.zeros_like(mark_ref)
    core = place_ref[0]
    half, step = rows_refs[0].shape[1], gate_ref.shape[1]
    ff = hidden_ref.shape[1]
    deltas = deltas_ref[...]
    copies = []
    for j in range(CORES):
        for at in range(0, half, step):
            n = (j * half + at) // step
            grad = dot(rows_refs[j][:, at : at + step], deltas, TN)
            gate_ref[n] = grad[:, :ff].astype(BF16)
            up_ref[n] = grad[:, ff:].astype(BF16)
            cols = columns((core ^ j) * half + at, step)
            copies += [
                pltpu.make_async_copy(gate_ref.at[n], gate_hbm.at[0, cols, :], sems.at[3 * n]),
                pltpu.make_async_copy(up_ref.at[n], up_hbm.at[0, cols, :], sems.at[3 * n + 1]),
            ]
            for copy in copies[-2:]:
                copy.start()
    hidden = hidden_ref[...].T
    for j in range(CORES):
        for at in range(0, half, step):
            n = (j * half + at) // step
            down_ref[n] = dot(hidden, grads_refs[j][:, at : at + step]).astype(BF16)
            cols = columns((core ^ j) * half + at, step)
            copies.append(pltpu.make_async_copy(down_ref.at[n], down_hbm.at[0, :, cols], sems.at[3 * n + 2]))
            copies[-1].start()
    for copy in copies:
        copy.wait()


def local(tokens, out_grad, combine, expert_ids, gate_weight, up_weight, down_weight):
    tok, width = tokens.shape
    chips = lax.axis_size(CHIPS)
    lines = chips * SLOTS
    ff = gate_weight.shape[2]
    half, quarter = width // CORES, width // CORES // 2
    step = 512
    place = lax.axis_index("core").astype(jnp.int32).reshape(1)

    def swap(x):
        return lax.ppermute(x, "core", [(0, 1), (1, 0)])

    def deliver(x):
        found = lax.all_to_all(x.reshape(chips, SLOTS, x.shape[1]), CHIPS, split_axis=0, concat_axis=0, tiled=True)
        return found.reshape(x.shape)

    ids, comb = expert_ids.T, combine.T
    ids_pair = (ids, swap(ids))
    tokens_pair = (tokens, swap(tokens))
    scratch = [pltpu.VMEM((half // step, lines, step), BF16), pltpu.SemaphoreType.DMA((half // step,))]
    out = ((lines, half), BF16)
    rows_out = call(
        build_kernel, "build_rows", [out], place, *ids_pair, *tokens_pair, direct=1, scratch=scratch, limit=63 << 20
    )[0]
    later = after(comb, out_grad, rows_out)[:2]
    comb_pair, out_grad_pair = [(x, swap(x)) for x in later]
    picks, grads_out = call(
        build_kernel, "build_grads", [(((TOPK + 1) * CORES * tok, lines), BF16), out],
        place, *ids_pair, *comb_pair, *out_grad_pair, direct=1, scratch=scratch, far=True,
    )
    lend = call(
        lend_kernel, "lend", [((half, 2 * ff), BF16)], place, gate_weight, up_weight, out_grad_pair[1],
        raw=3, scratch=[pltpu.SemaphoreType.DMA((2,))],
    )[0]
    back, parts_own = call(
        turn_kernel,
        "turn",
        [((width, ff), BF16), ((2 * ff, half), BF16)],
        place, gate_weight, up_weight, down_weight, out_grad_pair[1],
        raw=4,
        scratch=[pltpu.VMEM((half, 2 * ff), BF16), pltpu.VMEM((ff, width), BF16), pltpu.SemaphoreType.DMA((3,))],
    )
    rows, grads_out, back, parts_own, lend = after(deliver(rows_out), grads_out, back, parts_own, lend)
    parts_other = call(turn_lent_kernel, "turn_lent", [((2 * ff, half), BF16)], place, swap(lend))[0]
    rows_pair = (rows, swap(rows))
    factors, hidden = call(
        gate_up_kernel,
        "gate_up",
        [((lines, 2 * ff), F32), ((lines, ff), BF16)],
        place, gate_weight, up_weight, *rows_pair,
        raw=4,
        scratch=[
            pltpu.VMEM((4, lines, quarter), BF16),
            pltpu.VMEM((4, quarter, 2 * ff), BF16),
            pltpu.SemaphoreType.DMA((12,)),
        ],
    )
    grads, factors, hidden, parts_other = after(deliver(grads_out), factors, hidden, parts_other)
    grads_pair = (grads, swap(grads))
    scratch = [
        pltpu.VMEM((half // step, lines, step), BF16),
        pltpu.VMEM((half // step, step, ff), BF16),
        pltpu.SemaphoreType.DMA((2 * half // step,)),
    ]
    scaled = call(
        back_early_kernel, "back_early", [((lines, ff), F32)], place, back, grads, raw=2, scratch=scratch
    )[0]
    other, scaled = after(grads_pair[1], scaled)
    deltas, score = call(
        back_late_kernel,
        "back_late",
        [((lines, 2 * ff), BF16), ((lines, META), BF16)],
        place, back, other, scaled, factors, hidden, raw=2, scratch=scratch,
    )

    def parts(last, size, *args):
        return call(
            functools.partial(parts_kernel, last),
            "row_parts",
            [((lines, size), BF16)],
            place, *args,
            raw=1,
            direct=1,
            far=last,
            scratch=[
                pltpu.VMEM((half // step, 2 * ff, step), BF16),
                pltpu.VMEM((half // step, lines, step), BF16),
                pltpu.SemaphoreType.DMA((half // step,)),
                pltpu.SemaphoreType.DMA((half // step + 1,)),
            ],
        )[0]

    part = parts(False, half, parts_own, deltas)
    deltas_other, part = after(swap(deltas), part)
    parts_sum = parts(True, half + META, parts_other, deltas_other, part, score)
    mark, gate_grad, up_grad, down_grad = call(
        weights_kernel,
        "weight_grads",
        [((8, META), F32), (gate_weight.shape, BF16), (up_weight.shape, BF16), (down_weight.shape, BF16)],
        place, *rows_pair, *grads_pair, deltas, hidden,
        direct=3,
        scratch=[
            pltpu.VMEM((width // step, step, ff), BF16),
            pltpu.VMEM((width // step, step, ff), BF16),
            pltpu.VMEM((width // step, ff, step), BF16),
            pltpu.SemaphoreType.DMA((3 * width // step,)),
        ],
    )
    mine, send, mine_score, send_score = call(
        gather_kernel,
        "gather_rows",
        [((tok, half), BF16)] * CORES + [((TOPK, tok), F32)] * CORES,
        place, deliver(parts_sum), pltpu.with_memory_space_constraint(picks, pltpu.HBM), mark,
        raw=1,
        scratch=[pltpu.VMEM((half // step + 1, lines, step), BF16), pltpu.SemaphoreType.DMA((half // step + 1,))],
    )
    combine_grad = ((mine_score + swap(send_score)) / comb).T
    other = swap(send)
    token_grad = jnp.where(
        place[0] == 0, jnp.concatenate([mine, other], axis=1), jnp.concatenate([other, mine], axis=1)
    )
    return token_grad, combine_grad, gate_grad, up_grad, down_grad


def solution(mesh):
    outer, inner = mesh.devices.shape
    split = Mesh(mesh.devices.reshape(outer, inner // CORES, CORES), ALL)
    flat, deep = P(ALL, None), P(ALL, None, None)
    return jax.shard_map(
        local,
        mesh=split,
        in_specs=(flat, flat, flat, flat, deep, deep, deep),
        out_specs=(flat, flat, deep, deep, deep),
        check_vma=False,
    )
```

```python
import functools

import jax
import jax.numpy as jnp
from jax import lax
from jax.experimental import pallas as pl
from jax.experimental.pallas import tpu as pltpu
from jax.sharding import Mesh
from jax.sharding import PartitionSpec as P

CORES = 2
TOPK = 4
CAP = 4
SLOTS = CORES * CAP
META = 128
CHIPS = ("outer", "z")
ALL = ("outer", "z", "core")
F32 = jnp.float32
BF16 = jnp.bfloat16
TN = (((0,), (0,)), ((), ()))
NT = (((1,), (1,)), ((), ()))
SMEM = pl.BlockSpec(memory_space=pltpu.SMEM)
HBM = pl.BlockSpec(memory_space=pltpu.HBM)
VMEM = pl.BlockSpec(memory_space=pltpu.VMEM)


def dot(a, b, dims=(((1,), (0,)), ((), ()))):
    return lax.dot_general(a, b, dims, preferred_element_type=F32)


def after(x, *others):
    return lax.optimization_barrier((x, *others))


class Loaded:
    def __init__(self, source, target, semaphore):
        self.copy = pltpu.make_async_copy(source, target, semaphore)
        self.target = target
        self.shape = target.shape
        self.waiting = True
        self.copy.start()

    def wait(self):
        if self.waiting:
            self.copy.wait()
            self.waiting = False

    def __getitem__(self, index):
        self.wait()
        return self.target[index]


class Stages:
    def __init__(self, groups, depth):
        self.groups, self.depth = groups, depth
        for copy in sum(groups[:depth], []):
            copy.start()

    def wait(self, n):
        for copy in self.groups[n]:
            copy.wait()
        for copy in sum(self.groups[n + self.depth : n + self.depth + 1], []):
            copy.start()


def call(kernel, name, outs, place, *args, raw=0, direct=0, scratch=(), limit=28 << 20, far=False):
    count, given = len(outs) - direct, len(args) - raw

    def body(place_ref, *refs):
        raw_refs, ins, refs = refs[:raw], refs[raw : raw + given], refs[raw + given :]
        out_refs, direct_refs, refs = refs[:count], refs[count : count + direct], refs[count + direct :]
        held, made, refs = refs[:given], refs[given : given + count], refs[given + count :]
        in_sems, out_sems, own = refs[0], refs[1], refs[2:]
        loaded = [Loaded(ins[n], held[n], in_sems.at[n]) for n in range(given)]
        kernel(place_ref, *raw_refs, *loaded, *made, *direct_refs, *own)
        for held_ref in loaded:
            held_ref.wait()
        copies = [pltpu.make_async_copy(made[n], out_refs[n], out_sems.at[n]) for n in range(count)]
        for copy in copies:
            copy.start()
        for copy in copies:
            copy.wait()

    return pl.pallas_call(
        body,
        in_specs=[SMEM] + [HBM] * len(args),
        out_specs=[HBM] * len(outs),
        out_shape=[pltpu.HBM(*out) if far else jax.ShapeDtypeStruct(*out) for out in outs],
        scratch_shapes=[pltpu.VMEM(x.shape, x.dtype) for x in args[raw:]]
        + [pltpu.VMEM(shape, kind) for shape, kind in outs[:count]]
        + [pltpu.SemaphoreType.DMA((max(given, 1),)), pltpu.SemaphoreType.DMA((max(count, 1),)), *scratch],
        compiler_params=pltpu.CompilerParams(vmem_limit_bytes=limit),
        name=name,
    )(place, *args)


def call_near(kernel, name, outs, place, *args, direct=0, scratch=(), limit=28 << 20):
    count = len(outs) - direct
    return pl.pallas_call(
        kernel,
        in_specs=[SMEM] + [VMEM] * len(args),
        out_specs=[VMEM] * count + [HBM] * direct,
        out_shape=[jax.ShapeDtypeStruct(*out) for out in outs[:count]] + [pltpu.HBM(*out) for out in outs[count:]],
        scratch_shapes=list(scratch),
        compiler_params=pltpu.CompilerParams(vmem_limit_bytes=limit),
        name=name,
    )(place, *args)


def column(row):
    n = row.shape[1]
    here = lax.broadcasted_iota(jnp.int32, (n, n), 0) == lax.broadcasted_iota(jnp.int32, (n, n), 1)
    return jnp.sum(jnp.where(here, row, 0.0), axis=1, keepdims=True)


def row(column):
    n = column.shape[0]
    here = lax.broadcasted_iota(jnp.int32, (n, n), 0) == lax.broadcasted_iota(jnp.int32, (n, n), 1)
    return jnp.sum(jnp.where(here, column, 0.0), axis=0, keepdims=True)


def columns(start, size):
    return pl.ds(pl.multiple_of(start, size), size)


def slot_mask(core, ids, lines):
    tokens = ids[0].shape[0]
    own = tokens // CORES
    line = lax.broadcasted_iota(jnp.int32, (tokens, lines), 1)
    expert = (line // (2 * SLOTS)).astype(F32)
    named = [jnp.where(some == expert, 1.0, 0.0) for some in ids]
    total = named[0] + named[1] + named[2] + named[3]
    after = lax.broadcasted_iota(jnp.int32, (tokens, tokens), 0)
    before = lax.broadcasted_iota(jnp.int32, (tokens, tokens), 1)
    earlier = jnp.where((before < after) & (before // own == after // own), 1.0, 0.0)
    rank = dot(earlier.astype(BF16), total.astype(BF16)).astype(jnp.int32)
    token = lax.broadcasted_iota(jnp.int32, (tokens, lines), 0)
    place = rank + ((token // own) ^ core) * CAP
    mask = jnp.where((total > 0.0) & (place == line % SLOTS), 1.0, 0.0)
    return mask, named


def both_of(refs, k):
    return jnp.concatenate([column(ref[k : k + 1, :].astype(F32)) for ref in refs], axis=0)


def build_kernel(place_ref, ids_ref, other_ids_ref, *refs):
    scaled = len(refs) > 5
    if scaled:
        comb_refs, rows_refs, (picks_ref, out_hbm, out_ref, sems) = refs[0:2], refs[2:4], refs[4:]
    else:
        rows_refs, (out_hbm, out_ref, sems) = refs[0:2], refs[2:]
    core = place_ref[0]
    steps, lines, step = out_ref.shape
    tok, width = rows_refs[0].shape
    half = width // CORES
    ids_refs = (ids_ref, other_ids_ref)
    mask, named = slot_mask(core, [both_of(ids_refs, k) for k in range(TOPK)], lines)
    pick = mask.astype(BF16)
    if scaled:
        picks_ref[: CORES * tok, :] = pick
        for k in range(TOPK):
            picks_ref[(k + 1) * CORES * tok : (k + 2) * CORES * tok, :] = (mask * named[k]).astype(BF16)
        chosen = sum(named[k] * both_of(comb_refs, k) for k in range(TOPK)) * mask
        high = chosen.astype(BF16)
        ones = jnp.ones((mask.shape[0], META), BF16)
        weight = dot(high, ones, TN) + dot((chosen - high.astype(F32)).astype(BF16), ones, TN)
        weight = weight[:, :1]
    copies = []
    for n in range(steps):
        cols = columns(core * half + n * step, step)
        found = dot(pick, jnp.concatenate([ref[:, cols] for ref in rows_refs], axis=0), TN)
        out_ref[n] = (found * weight if scaled else found).astype(BF16)
        copies.append(pltpu.make_async_copy(out_ref.at[n], out_hbm.at[:, pl.ds(n * step, step)], sems.at[n]))
        copies[-1].start()
    for copy in copies:
        copy.wait()


def lend_kernel(place_ref, gate_hbm, up_hbm, order_hbm, first_ref, sems):
    half, both = first_ref.shape
    ff = both // 2
    at = columns((1 - place_ref[0]) * half, half)
    copies = [
        pltpu.make_async_copy(gate_hbm.at[0, at, :], first_ref.at[:, pl.ds(0, ff)], sems.at[0]),
        pltpu.make_async_copy(up_hbm.at[0, at, :], first_ref.at[:, pl.ds(ff, ff)], sems.at[1]),
    ]
    for copy in copies:
        copy.start()
    for copy in copies:
        copy.wait()


def turn_kernel(place_ref, gate_hbm, up_hbm, down_hbm, order_hbm, back_ref, parts_ref, first_ref, down_ref, sems):
    half, both = first_ref.shape
    ff = both // 2
    at = columns(place_ref[0] * half, half)
    copies = [
        pltpu.make_async_copy(down_hbm.at[0], down_ref, sems.at[0]),
        pltpu.make_async_copy(gate_hbm.at[0, at, :], first_ref.at[:, pl.ds(0, ff)], sems.at[1]),
        pltpu.make_async_copy(up_hbm.at[0, at, :], first_ref.at[:, pl.ds(ff, ff)], sems.at[2]),
    ]
    for copy in copies:
        copy.start()
    for copy in copies:
        copy.wait()
    step = 256
    for n in range(0, CORES * half, step):
        back_ref[n : n + step, :] = down_ref[:, n : n + step].T
    for n in range(0, half, step):
        parts_ref[:, n : n + step] = first_ref[n : n + step, :].T


def turn_lent_kernel(place_ref, lent_ref, parts_ref):
    step = 256
    for n in range(0, lent_ref.shape[0], step):
        parts_ref[:, n : n + step] = lent_ref[n : n + step, :].T


def gate_up_kernel(place_ref, gate_hbm, up_hbm, own_hbm, other_hbm, factors_ref, hidden_ref, rows_ref, first_ref, sems):
    core = place_ref[0]
    parts, step, both = first_ref.shape
    ff = both // 2
    half = parts * step // CORES
    groups = []
    for n in range(parts):
        j, at = divmod(n * step, half)
        cols = columns((core ^ j) * half + at, step)
        pairs = (
            ((own_hbm, other_hbm)[j].at[:, pl.ds(at, step)], rows_ref.at[n]),
            (gate_hbm.at[0, cols, :], first_ref.at[n, :, pl.ds(0, ff)]),
            (up_hbm.at[0, cols, :], first_ref.at[n, :, pl.ds(ff, ff)]),
        )
        groups.append([pltpu.make_async_copy(*pair, sems.at[3 * n + k]) for k, pair in enumerate(pairs)])
    stages = Stages(groups, 2)
    pre = 0.0
    for n in range(parts):
        stages.wait(n)
        pre += dot(rows_ref[n], first_ref[n])
    gate_pre, up_pre = pre[:, :ff], pre[:, ff:]
    sigmoid_gate = jax.nn.sigmoid(gate_pre)
    active = gate_pre * sigmoid_gate
    hidden_ref[...] = (active * up_pre).astype(BF16)
    factors_ref[:, :ff] = up_pre * sigmoid_gate * (1.0 + gate_pre * (1.0 - sigmoid_gate))
    factors_ref[:, ff:] = active


def back_product(which, back_ref, grads_ref):
    half = grads_ref.shape[1]
    return dot(grads_ref[...], back_ref[columns(which * half, half), :])


def back_early_kernel(place_ref, back_ref, own_ref, out_ref):
    out_ref[...] = back_product(place_ref[0], back_ref, own_ref)


def back_late_kernel(place_ref, back_ref, other_ref, sum_ref, factors_ref, hidden_ref, deltas_ref, score_ref):
    scaled = back_product(1 - place_ref[0], back_ref, other_ref) + sum_ref[...]
    ff = scaled.shape[1]
    score = jnp.sum(scaled * hidden_ref[...].astype(F32), axis=1, keepdims=True)
    deltas_ref[:, :ff] = (scaled * factors_ref[:, :ff]).astype(BF16)
    deltas_ref[:, ff:] = (scaled * factors_ref[:, ff:]).astype(BF16)
    score_ref[...] = jnp.broadcast_to(score, score_ref.shape).astype(BF16)


def parts_own_kernel(place_ref, turned_ref, deltas_ref, out_ref):
    step = 512
    deltas = deltas_ref[...]
    for at in range(0, out_ref.shape[1], step):
        out_ref[:, at : at + step] = dot(deltas, turned_ref[:, at : at + step]).astype(BF16)


def parts_sum_kernel(place_ref, turned_ref, deltas_ref, before_ref, score_ref, out_hbm, part_ref, sems):
    steps, _, step = part_ref.shape
    half = steps * step
    outs = [pltpu.make_async_copy(score_ref, out_hbm.at[:, pl.ds(half, META)], sems.at[steps])]
    outs[0].start()
    deltas = deltas_ref[...]
    for n in range(steps):
        at = n * step
        part = dot(deltas, turned_ref[:, at : at + step]) + before_ref[:, at : at + step].astype(F32)
        part_ref[n] = part.astype(BF16)
        outs.append(pltpu.make_async_copy(part_ref.at[n], out_hbm.at[:, pl.ds(at, step)], sems.at[n]))
        outs[-1].start()
    for copy in outs:
        copy.wait()


def gather_kernel(place_ref, back_hbm, picks_ref, mark_ref, mine_ref, send_ref, mine_score_ref, send_score_ref, back_ref, sems):
    tok, width = mine_ref.shape
    tokens = CORES * tok
    steps, _, step = back_ref.shape
    copies = [pltpu.make_async_copy(back_hbm.at[:, pl.ds(width, META)], back_ref.at[steps - 1, :, pl.ds(0, META)], sems.at[0])]
    for n in range(steps - 1):
        copies.append(pltpu.make_async_copy(back_hbm.at[:, pl.ds(n * step, step)], back_ref.at[n], sems.at[n + 1]))
    for copy in copies:
        copy.start()
    pick = picks_ref[:tokens, :]
    copies[0].wait()
    scores = dot(picks_ref[tokens:, :], back_ref[steps - 1, :, :META])
    for k in range(TOPK):
        mine_score_ref[k : k + 1, :] = row(scores[k * tokens : k * tokens + tok, :1])
        send_score_ref[k : k + 1, :] = row(scores[k * tokens + tok : (k + 1) * tokens, :1])
    for n in range(steps - 1):
        copies[n + 1].wait()
        part = dot(pick, back_ref[n]).astype(BF16)
        mine_ref[:, n * step : (n + 1) * step] = part[:tok]
        send_ref[:, n * step : (n + 1) * step] = part[tok:]


def weights_kernel(place_ref, *refs):
    rows_refs, grads_refs = refs[0:2], refs[2:4]
    deltas_ref, hidden_ref, mark_ref, gate_hbm, up_hbm, down_hbm, gate_ref, up_ref, down_ref, sems = refs[4:]
    mark_ref[...] = jnp.zeros_like(mark_ref)
    core = place_ref[0]
    half, step = rows_refs[0].shape[1], gate_ref.shape[1]
    ff = hidden_ref.shape[1]
    deltas = deltas_ref[...]
    copies = []
    for j in range(CORES):
        for at in range(0, half, step):
            n = (j * half + at) // step
            grad = dot(rows_refs[j][:, at : at + step], deltas, TN)
            gate_ref[n] = grad[:, :ff].astype(BF16)
            up_ref[n] = grad[:, ff:].astype(BF16)
            cols = columns((core ^ j) * half + at, step)
            copies += [
                pltpu.make_async_copy(gate_ref.at[n], gate_hbm.at[0, cols, :], sems.at[3 * n]),
                pltpu.make_async_copy(up_ref.at[n], up_hbm.at[0, cols, :], sems.at[3 * n + 1]),
            ]
            for copy in copies[-2:]:
                copy.start()
    hidden = hidden_ref[...].T
    for j in range(CORES):
        for at in range(0, half, step):
            n = (j * half + at) // step
            down_ref[n] = dot(hidden, grads_refs[j][:, at : at + step]).astype(BF16)
            cols = columns((core ^ j) * half + at, step)
            copies.append(pltpu.make_async_copy(down_ref.at[n], down_hbm.at[0, :, cols], sems.at[3 * n + 2]))
            copies[-1].start()
    for copy in copies:
        copy.wait()


def local(tokens, out_grad, combine, expert_ids, gate_weight, up_weight, down_weight):
    tok, width = tokens.shape
    chips = lax.axis_size(CHIPS)
    lines = chips * SLOTS
    ff = gate_weight.shape[2]
    half, quarter = width // CORES, width // CORES // 2
    step = 512
    place = lax.axis_index("core").astype(jnp.int32).reshape(1)

    def swap(x):
        return lax.ppermute(x, "core", [(0, 1), (1, 0)])

    def deliver(x):
        found = lax.all_to_all(x.reshape(chips, SLOTS, x.shape[1]), CHIPS, split_axis=0, concat_axis=0, tiled=True)
        return found.reshape(x.shape)

    ids, comb = expert_ids.T, combine.T
    ids_pair = (ids, swap(ids))
    tokens_pair = (tokens, swap(tokens))
    scratch = [pltpu.VMEM((half // step, lines, step), BF16), pltpu.SemaphoreType.DMA((half // step,))]
    out = ((lines, half), BF16)
    rows_out = call(
        build_kernel, "build_rows", [out], place, *[pltpu.with_memory_space_constraint(x, pltpu.HBM) for x in ids_pair],
        pltpu.with_memory_space_constraint(tokens, pltpu.HBM), tokens_pair[1], direct=1, scratch=scratch, far=True,
    )[0]
    later = after(comb, out_grad, rows_out)[:2]
    comb_pair, out_grad_pair = [(x, swap(x)) for x in later]
    picks, grads_out = call(
        build_kernel, "build_grads", [(((TOPK + 1) * CORES * tok, lines), BF16), out],
        place, *ids_pair, *comb_pair, *out_grad_pair, direct=1, scratch=scratch, far=True,
    )
    lend = call(
        lend_kernel, "lend", [((half, 2 * ff), BF16)], place, gate_weight, up_weight, out_grad_pair[1],
        raw=3, scratch=[pltpu.SemaphoreType.DMA((2,))],
    )[0]
    back, parts_own = call(
        turn_kernel,
        "turn",
        [((width, ff), BF16), ((2 * ff, half), BF16)],
        place, gate_weight, up_weight, down_weight, out_grad_pair[1],
        raw=4,
        scratch=[pltpu.VMEM((half, 2 * ff), BF16), pltpu.VMEM((ff, width), BF16), pltpu.SemaphoreType.DMA((3,))],
    )
    rows, grads_out, back, parts_own, lend = after(deliver(rows_out), grads_out, back, parts_own, lend)
    parts_other = call(turn_lent_kernel, "turn_lent", [((2 * ff, half), BF16)], place, swap(lend))[0]
    rows_pair = (rows, swap(rows))
    factors, hidden = call(
        gate_up_kernel,
        "gate_up",
        [((lines, 2 * ff), F32), ((lines, ff), BF16)],
        place, gate_weight, up_weight, *rows_pair,
        raw=4,
        scratch=[
            pltpu.VMEM((4, lines, quarter), BF16),
            pltpu.VMEM((4, quarter, 2 * ff), BF16),
            pltpu.SemaphoreType.DMA((12,)),
        ],
    )
    grads, factors, hidden, parts_other = after(deliver(grads_out), factors, hidden, parts_other)
    grads_pair = (grads, swap(grads))
    scaled = call_near(back_early_kernel, "back_early", [((lines, ff), F32)], place, back, grads)[0]
    other, scaled = after(grads_pair[1], scaled)
    deltas, score = call_near(
        back_late_kernel,
        "back_late",
        [((lines, 2 * ff), BF16), ((lines, META), BF16)],
        place, back, other, scaled, factors, hidden,
    )
    part = call_near(parts_own_kernel, "parts_own", [((lines, half), BF16)], place, parts_own, deltas)[0]
    deltas_other, part = after(swap(deltas), part)
    parts_sum = call_near(
        parts_sum_kernel,
        "parts_sum",
        [((lines, half + META), BF16)],
        place, parts_other, deltas_other, part, score,
        direct=1,
        scratch=[pltpu.VMEM((half // step, lines, step), BF16), pltpu.SemaphoreType.DMA((half // step + 1,))],
    )[0]
    mark, gate_grad, up_grad, down_grad = call(
        weights_kernel,
        "weight_grads",
        [((8, META), F32), (gate_weight.shape, BF16), (up_weight.shape, BF16), (down_weight.shape, BF16)],
        place, *rows_pair, *grads_pair, deltas, hidden,
        direct=3,
        scratch=[
            pltpu.VMEM((width // step, step, ff), BF16),
            pltpu.VMEM((width // step, step, ff), BF16),
            pltpu.VMEM((width // step, ff, step), BF16),
            pltpu.SemaphoreType.DMA((3 * width // step,)),
        ],
    )
    mine, send, mine_score, send_score = call(
        gather_kernel,
        "gather_rows",
        [((tok, half), BF16)] * CORES + [((TOPK, tok), F32)] * CORES,
        place, deliver(parts_sum), pltpu.with_memory_space_constraint(picks, pltpu.HBM), mark,
        raw=1,
        scratch=[pltpu.VMEM((half // step + 1, lines, step), BF16), pltpu.SemaphoreType.DMA((half // step + 1,))],
    )
    combine_grad = ((mine_score + swap(send_score)) / comb).T
    other = swap(send)
    token_grad = jnp.where(
        place[0] == 0, jnp.concatenate([mine, other], axis=1), jnp.concatenate([other, mine], axis=1)
    )
    return token_grad, combine_grad, gate_grad, up_grad, down_grad


def solution(mesh):
    outer, inner = mesh.devices.shape
    split = Mesh(mesh.devices.reshape(outer, inner // CORES, CORES), ALL)
    flat, deep = P(ALL, None), P(ALL, None, None)
    return jax.shard_map(
        local,
        mesh=split,
        in_specs=(flat, flat, flat, flat, deep, deep, deep),
        out_specs=(flat, flat, deep, deep, deep),
        check_vma=False,
    )
```

```python
import functools

import jax
import jax.numpy as jnp
from jax import lax
from jax.experimental import pallas as pl
from jax.experimental.pallas import tpu as pltpu
from jax.sharding import Mesh
from jax.sharding import PartitionSpec as P

CORES = 2
TOPK = 4
CAP = 4
SLOTS = CORES * CAP
META = 128
CHIPS = ("outer", "z")
ALL = ("outer", "z", "core")
F32 = jnp.float32
BF16 = jnp.bfloat16
TN = (((0,), (0,)), ((), ()))
NT = (((1,), (1,)), ((), ()))
SMEM = pl.BlockSpec(memory_space=pltpu.SMEM)
HBM = pl.BlockSpec(memory_space=pltpu.HBM)
VMEM = pl.BlockSpec(memory_space=pltpu.VMEM)


def dot(a, b, dims=(((1,), (0,)), ((), ()))):
    return lax.dot_general(a, b, dims, preferred_element_type=F32)


def after(x, *others):
    return lax.optimization_barrier((x, *others))


class Loaded:
    def __init__(self, source, target, semaphore):
        self.copy = pltpu.make_async_copy(source, target, semaphore)
        self.target = target
        self.shape = target.shape
        self.waiting = True
        self.copy.start()

    def wait(self):
        if self.waiting:
            self.copy.wait()
            self.waiting = False

    def __getitem__(self, index):
        self.wait()
        return self.target[index]


class Stages:
    def __init__(self, groups, depth):
        self.groups, self.depth = groups, depth
        for copy in sum(groups[:depth], []):
            copy.start()

    def wait(self, n):
        for copy in self.groups[n]:
            copy.wait()
        for copy in sum(self.groups[n + self.depth : n + self.depth + 1], []):
            copy.start()


def call(kernel, name, outs, place, *args, raw=0, direct=0, near=0, scratch=(), limit=28 << 20, far=False):
    count, given = len(outs) - direct, len(args) - raw - near

    def body(place_ref, *refs):
        raw_refs, ins, refs = refs[:raw], refs[raw : raw + given], refs[raw + given :]
        near_refs, refs = refs[:near], refs[near:]
        out_refs, direct_refs, refs = refs[:count], refs[count : count + direct], refs[count + direct :]
        held, made, refs = refs[:given], refs[given : given + count], refs[given + count :]
        in_sems, out_sems, own = refs[0], refs[1], refs[2:]
        loaded = [Loaded(ins[n], held[n], in_sems.at[n]) for n in range(given)]
        kernel(place_ref, *raw_refs, *loaded, *near_refs, *made, *direct_refs, *own)
        for held_ref in loaded:
            held_ref.wait()
        copies = [pltpu.make_async_copy(made[n], out_refs[n], out_sems.at[n]) for n in range(count)]
        for copy in copies:
            copy.start()
        for copy in copies:
            copy.wait()

    return pl.pallas_call(
        body,
        in_specs=[SMEM] + [HBM] * (raw + given) + [VMEM] * near,
        out_specs=[HBM] * len(outs),
        out_shape=[pltpu.HBM(*out) if far else jax.ShapeDtypeStruct(*out) for out in outs],
        scratch_shapes=[pltpu.VMEM(x.shape, x.dtype) for x in args[raw : raw + given]]
        + [pltpu.VMEM(shape, kind) for shape, kind in outs[:count]]
        + [pltpu.SemaphoreType.DMA((max(given, 1),)), pltpu.SemaphoreType.DMA((max(count, 1),)), *scratch],
        compiler_params=pltpu.CompilerParams(vmem_limit_bytes=limit),
        name=name,
    )(place, *args)


def call_near(kernel, name, outs, place, *args, direct=0, scratch=(), limit=28 << 20):
    count = len(outs) - direct
    return pl.pallas_call(
        kernel,
        in_specs=[SMEM] + [VMEM] * len(args),
        out_specs=[VMEM] * count + [HBM] * direct,
        out_shape=[jax.ShapeDtypeStruct(*out) for out in outs[:count]] + [pltpu.HBM(*out) for out in outs[count:]],
        scratch_shapes=list(scratch),
        compiler_params=pltpu.CompilerParams(vmem_limit_bytes=limit),
        name=name,
    )(place, *args)


def column(row):
    n = row.shape[1]
    here = lax.broadcasted_iota(jnp.int32, (n, n), 0) == lax.broadcasted_iota(jnp.int32, (n, n), 1)
    return jnp.sum(jnp.where(here, row, 0.0), axis=1, keepdims=True)


def row(column):
    n = column.shape[0]
    here = lax.broadcasted_iota(jnp.int32, (n, n), 0) == lax.broadcasted_iota(jnp.int32, (n, n), 1)
    return jnp.sum(jnp.where(here, column, 0.0), axis=0, keepdims=True)


def columns(start, size):
    return pl.ds(pl.multiple_of(start, size), size)


def slot_mask(core, ids, lines):
    tokens = ids[0].shape[0]
    own = tokens // CORES
    line = lax.broadcasted_iota(jnp.int32, (tokens, lines), 1)
    expert = (line // (2 * SLOTS)).astype(F32)
    named = [jnp.where(some == expert, 1.0, 0.0) for some in ids]
    total = named[0] + named[1] + named[2] + named[3]
    after = lax.broadcasted_iota(jnp.int32, (tokens, tokens), 0)
    before = lax.broadcasted_iota(jnp.int32, (tokens, tokens), 1)
    earlier = jnp.where((before < after) & (before // own == after // own), 1.0, 0.0)
    rank = dot(earlier.astype(BF16), total.astype(BF16)).astype(jnp.int32)
    token = lax.broadcasted_iota(jnp.int32, (tokens, lines), 0)
    place = rank + ((token // own) ^ core) * CAP
    mask = jnp.where((total > 0.0) & (place == line % SLOTS), 1.0, 0.0)
    return mask, named


def both_of(refs, k):
    return jnp.concatenate([column(ref[k : k + 1, :].astype(F32)) for ref in refs], axis=0)


def build_kernel(place_ref, ids_ref, other_ids_ref, *refs):
    scaled = len(refs) > 5
    if scaled:
        comb_refs, rows_refs, (picks_ref, out_hbm, out_ref, sems) = refs[0:2], refs[2:4], refs[4:]
    else:
        rows_refs, (out_hbm, out_ref, sems) = refs[0:2], refs[2:]
    core = place_ref[0]
    steps, lines, step = out_ref.shape
    tok, width = rows_refs[0].shape
    half = width // CORES
    ids_refs = (ids_ref, other_ids_ref)
    mask, named = slot_mask(core, [both_of(ids_refs, k) for k in range(TOPK)], lines)
    pick = mask.astype(BF16)
    if scaled:
        picks_ref[: CORES * tok, :] = pick
        for k in range(TOPK):
            picks_ref[(k + 1) * CORES * tok : (k + 2) * CORES * tok, :] = (mask * named[k]).astype(BF16)
        chosen = sum(named[k] * both_of(comb_refs, k) for k in range(TOPK)) * mask
        high = chosen.astype(BF16)
        ones = jnp.ones((mask.shape[0], META), BF16)
        weight = dot(high, ones, TN) + dot((chosen - high.astype(F32)).astype(BF16), ones, TN)
        weight = weight[:, :1]
    copies = []
    for n in range(steps):
        cols = columns(core * half + n * step, step)
        found = dot(pick, jnp.concatenate([ref[:, cols] for ref in rows_refs], axis=0), TN)
        out_ref[n] = (found * weight if scaled else found).astype(BF16)
        copies.append(pltpu.make_async_copy(out_ref.at[n], out_hbm.at[:, pl.ds(n * step, step)], sems.at[n]))
        copies[-1].start()
    for copy in copies:
        copy.wait()


def build_rows_kernel(place_ref, ids_ref, rows_ref, other_ids_ref, other_rows_ref, *refs):
    build_kernel(place_ref, ids_ref, other_ids_ref, rows_ref, other_rows_ref, *refs)


def lend_kernel(place_ref, gate_hbm, up_hbm, order_hbm, first_ref, sems):
    half, both = first_ref.shape
    ff = both // 2
    at = columns((1 - place_ref[0]) * half, half)
    copies = [
        pltpu.make_async_copy(gate_hbm.at[0, at, :], first_ref.at[:, pl.ds(0, ff)], sems.at[0]),
        pltpu.make_async_copy(up_hbm.at[0, at, :], first_ref.at[:, pl.ds(ff, ff)], sems.at[1]),
    ]
    for copy in copies:
        copy.start()
    for copy in copies:
        copy.wait()


def turn_kernel(place_ref, gate_ref, up_ref, down_ref, lent_ref, back_ref, own_ref, other_ref):
    half = lent_ref.shape[0]
    ff, width = down_ref.shape[1:]
    step = 256
    for n in range(0, width, step):
        back_ref[n : n + step, :] = down_ref[0, :, n : n + step].T
    for n in range(0, half, step):
        at = columns(place_ref[0] * half + n, step)
        own_ref[:ff, n : n + step] = gate_ref[0, at, :].T
        own_ref[ff:, n : n + step] = up_ref[0, at, :].T
        other_ref[:, n : n + step] = lent_ref[n : n + step, :].T


def gate_up_kernel(place_ref, gate_hbm, up_hbm, own_hbm, other_hbm, factors_ref, hidden_ref, rows_ref, first_ref, sems):
    core = place_ref[0]
    parts, step, both = first_ref.shape
    ff = both // 2
    half = parts * step // CORES
    groups = []
    for n in range(parts):
        j, at = divmod(n * step, half)
        cols = columns((core ^ j) * half + at, step)
        pairs = (
            ((own_hbm, other_hbm)[j].at[:, pl.ds(at, step)], rows_ref.at[n]),
            (gate_hbm.at[0, cols, :], first_ref.at[n, :, pl.ds(0, ff)]),
            (up_hbm.at[0, cols, :], first_ref.at[n, :, pl.ds(ff, ff)]),
        )
        groups.append([pltpu.make_async_copy(*pair, sems.at[3 * n + k]) for k, pair in enumerate(pairs)])
    stages = Stages(groups, 2)
    pre = 0.0
    for n in range(parts):
        stages.wait(n)
        pre += dot(rows_ref[n], first_ref[n])
    gate_pre, up_pre = pre[:, :ff], pre[:, ff:]
    sigmoid_gate = jax.nn.sigmoid(gate_pre)
    active = gate_pre * sigmoid_gate
    hidden_ref[...] = (active * up_pre).astype(BF16)
    factors_ref[:, :ff] = up_pre * sigmoid_gate * (1.0 + gate_pre * (1.0 - sigmoid_gate))
    factors_ref[:, ff:] = active


def back_product(which, back_ref, grads_ref):
    half = grads_ref.shape[1]
    return dot(grads_ref[...], back_ref[columns(which * half, half), :])


def back_early_kernel(place_ref, back_ref, own_ref, out_ref):
    out_ref[...] = back_product(place_ref[0], back_ref, own_ref)


def back_late_kernel(place_ref, back_ref, other_ref, sum_ref, factors_ref, hidden_ref, deltas_ref, score_ref):
    scaled = back_product(1 - place_ref[0], back_ref, other_ref) + sum_ref[...]
    ff = scaled.shape[1]
    score = jnp.sum(scaled * hidden_ref[...].astype(F32), axis=1, keepdims=True)
    deltas_ref[:, :ff] = (scaled * factors_ref[:, :ff]).astype(BF16)
    deltas_ref[:, ff:] = (scaled * factors_ref[:, ff:]).astype(BF16)
    score_ref[...] = jnp.broadcast_to(score, score_ref.shape).astype(BF16)


def parts_own_kernel(place_ref, turned_ref, deltas_ref, out_ref):
    step = 512
    deltas = deltas_ref[...]
    for at in range(0, out_ref.shape[1], step):
        out_ref[:, at : at + step] = dot(deltas, turned_ref[:, at : at + step]).astype(BF16)


def parts_sum_kernel(place_ref, turned_ref, deltas_ref, before_ref, score_ref, out_hbm, part_ref, sems):
    steps, _, step = part_ref.shape
    half = steps * step
    outs = [pltpu.make_async_copy(score_ref, out_hbm.at[:, pl.ds(half, META)], sems.at[steps])]
    outs[0].start()
    deltas = deltas_ref[...]
    for n in range(steps):
        at = n * step
        part = dot(deltas, turned_ref[:, at : at + step]) + before_ref[:, at : at + step].astype(F32)
        part_ref[n] = part.astype(BF16)
        outs.append(pltpu.make_async_copy(part_ref.at[n], out_hbm.at[:, pl.ds(at, step)], sems.at[n]))
        outs[-1].start()
    for copy in outs:
        copy.wait()


def gather_kernel(place_ref, back_ref, picks_ref, mine_ref, send_ref, mine_score_ref, send_score_ref):
    tok, width = mine_ref.shape
    tokens = CORES * tok
    step = 512
    pick = picks_ref[:tokens, :]
    for at in range(0, width, step):
        part = dot(pick, back_ref[:, at : at + step]).astype(BF16)
        mine_ref[:, at : at + step] = part[:tok]
        send_ref[:, at : at + step] = part[tok:]
    scores = dot(picks_ref[tokens:, :], back_ref[:, width:])
    for k in range(TOPK):
        mine_score_ref[k : k + 1, :] = row(scores[k * tokens : k * tokens + tok, :1])
        send_score_ref[k : k + 1, :] = row(scores[k * tokens + tok : (k + 1) * tokens, :1])


def weights_kernel(place_ref, *refs):
    rows_refs, grads_refs = refs[0:2], refs[2:4]
    deltas_ref, hidden_ref, given_ref, picks_ref, gate_hbm, up_hbm, down_hbm, gate_ref, up_ref, down_ref, sems = refs[4:]
    picks_ref[...] = given_ref[...]
    core = place_ref[0]
    half, step = rows_refs[0].shape[1], gate_ref.shape[1]
    ff = hidden_ref.shape[1]
    deltas = deltas_ref[...]
    copies = []
    for j in range(CORES):
        for at in range(0, half, step):
            n = (j * half + at) // step
            grad = dot(rows_refs[j][:, at : at + step], deltas, TN)
            gate_ref[n] = grad[:, :ff].astype(BF16)
            up_ref[n] = grad[:, ff:].astype(BF16)
            cols = columns((core ^ j) * half + at, step)
            copies += [
                pltpu.make_async_copy(gate_ref.at[n], gate_hbm.at[0, cols, :], sems.at[3 * n]),
                pltpu.make_async_copy(up_ref.at[n], up_hbm.at[0, cols, :], sems.at[3 * n + 1]),
            ]
            for copy in copies[-2:]:
                copy.start()
    hidden = hidden_ref[...].T
    for j in range(CORES):
        for at in range(0, half, step):
            n = (j * half + at) // step
            down_ref[n] = dot(hidden, grads_refs[j][:, at : at + step]).astype(BF16)
            cols = columns((core ^ j) * half + at, step)
            copies.append(pltpu.make_async_copy(down_ref.at[n], down_hbm.at[0, :, cols], sems.at[3 * n + 2]))
            copies[-1].start()
    for copy in copies:
        copy.wait()


def local(tokens, out_grad, combine, expert_ids, gate_weight, up_weight, down_weight):
    tok, width = tokens.shape
    chips = lax.axis_size(CHIPS)
    lines = chips * SLOTS
    ff = gate_weight.shape[2]
    half, quarter = width // CORES, width // CORES // 2
    step = 512
    place = lax.axis_index("core").astype(jnp.int32).reshape(1)

    def swap(x):
        return lax.ppermute(x, "core", [(0, 1), (1, 0)])

    def deliver(x):
        found = lax.all_to_all(x.reshape(chips, SLOTS, x.shape[1]), CHIPS, split_axis=0, concat_axis=0, tiled=True)
        return found.reshape(x.shape)

    ids, comb = expert_ids.T, combine.T
    ids_pair = (ids, swap(ids))
    tokens_pair = (tokens, swap(tokens))
    scratch = [pltpu.VMEM((half // step, lines, step), BF16), pltpu.SemaphoreType.DMA((half // step,))]
    out = ((lines, half), BF16)
    rows_out = call(
        build_rows_kernel, "build_rows", [out],
        place, *[pltpu.with_memory_space_constraint(x, pltpu.HBM) for x in (ids, tokens)], ids_pair[1], tokens_pair[1],
        direct=1, near=2, scratch=scratch, far=True,
    )[0]
    later = after(comb, out_grad, rows_out)[:2]
    comb_pair, out_grad_pair = [(x, swap(x)) for x in later]
    picks, grads_out = call(
        build_kernel, "build_grads", [(((TOPK + 1) * CORES * tok, lines), BF16), out],
        place, *ids_pair, *comb_pair, *out_grad_pair, direct=1, scratch=scratch, far=True,
    )
    lend = call(
        lend_kernel, "lend", [((half, 2 * ff), BF16)], place, gate_weight, up_weight, out_grad_pair[1],
        raw=3, scratch=[pltpu.SemaphoreType.DMA((2,))],
    )[0]
    rows, grads_out, lend = after(deliver(rows_out), grads_out, lend)
    back, parts_own, parts_other = call_near(
        turn_kernel,
        "turn",
        [((width, ff), BF16)] + [((2 * ff, half), BF16)] * CORES,
        place, gate_weight, up_weight, down_weight, swap(lend),
    )
    rows_pair = (rows, swap(rows))
    factors, hidden = call(
        gate_up_kernel,
        "gate_up",
        [((lines, 2 * ff), F32), ((lines, ff), BF16)],
        place, gate_weight, up_weight, *rows_pair,
        raw=4,
        scratch=[
            pltpu.VMEM((4, lines, quarter), BF16),
            pltpu.VMEM((4, quarter, 2 * ff), BF16),
            pltpu.SemaphoreType.DMA((12,)),
        ],
    )
    grads, factors, hidden, back, parts_own, parts_other = after(
        deliver(grads_out), factors, hidden, back, parts_own, parts_other
    )
    grads_pair = (grads, swap(grads))
    scaled = call_near(back_early_kernel, "back_early", [((lines, ff), F32)], place, back, grads)[0]
    other, scaled = after(grads_pair[1], scaled)
    deltas, score = call_near(
        back_late_kernel,
        "back_late",
        [((lines, 2 * ff), BF16), ((lines, META), BF16)],
        place, back, other, scaled, factors, hidden,
    )
    part = call_near(parts_own_kernel, "parts_own", [((lines, half), BF16)], place, parts_own, deltas)[0]
    deltas_other, part = after(swap(deltas), part)
    parts_sum = call_near(
        parts_sum_kernel,
        "parts_sum",
        [((lines, half + META), BF16)],
        place, parts_other, deltas_other, part, score,
        direct=1,
        scratch=[pltpu.VMEM((half // step, lines, step), BF16), pltpu.SemaphoreType.DMA((half // step + 1,))],
    )[0]
    picks, gate_grad, up_grad, down_grad = call(
        weights_kernel,
        "weight_grads",
        [(picks.shape, BF16), (gate_weight.shape, BF16), (up_weight.shape, BF16), (down_weight.shape, BF16)],
        place, *rows_pair, *grads_pair, deltas, hidden, picks,
        direct=3,
        scratch=[
            pltpu.VMEM((width // step, step, ff), BF16),
            pltpu.VMEM((width // step, step, ff), BF16),
            pltpu.VMEM((width // step, ff, step), BF16),
            pltpu.SemaphoreType.DMA((3 * width // step,)),
        ],
    )
    mine, send, mine_score, send_score = call_near(
        gather_kernel,
        "gather_rows",
        [((tok, half), BF16)] * CORES + [((TOPK, tok), F32)] * CORES,
        place, deliver(parts_sum), picks,
    )
    combine_grad = ((mine_score + swap(send_score)) / comb).T
    other = swap(send)
    token_grad = jnp.where(
        place[0] == 0, jnp.concatenate([mine, other], axis=1), jnp.concatenate([other, mine], axis=1)
    )
    return token_grad, combine_grad, gate_grad, up_grad, down_grad


def solution(mesh):
    outer, inner = mesh.devices.shape
    split = Mesh(mesh.devices.reshape(outer, inner // CORES, CORES), ALL)
    flat, deep = P(ALL, None), P(ALL, None, None)
    return jax.shard_map(
        local,
        mesh=split,
        in_specs=(flat, flat, flat, flat, deep, deep, deep),
        out_specs=(flat, flat, deep, deep, deep),
        check_vma=False,
    )
```

```python
import functools

import jax
import jax.numpy as jnp
from jax import lax
from jax.experimental import pallas as pl
from jax.experimental.pallas import tpu as pltpu
from jax.sharding import Mesh
from jax.sharding import PartitionSpec as P

CORES = 2
TOPK = 4
CAP = 4
SLOTS = CORES * CAP
META = 128
CHIPS = ("outer", "z")
ALL = ("outer", "z", "core")
F32 = jnp.float32
BF16 = jnp.bfloat16
TN = (((0,), (0,)), ((), ()))
NT = (((1,), (1,)), ((), ()))
SMEM = pl.BlockSpec(memory_space=pltpu.SMEM)
HBM = pl.BlockSpec(memory_space=pltpu.HBM)
VMEM = pl.BlockSpec(memory_space=pltpu.VMEM)


def dot(a, b, dims=(((1,), (0,)), ((), ()))):
    return lax.dot_general(a, b, dims, preferred_element_type=F32)


def after(x, *others):
    return lax.optimization_barrier((x, *others))


class Loaded:
    def __init__(self, source, target, semaphore):
        self.copy = pltpu.make_async_copy(source, target, semaphore)
        self.target = target
        self.shape = target.shape
        self.waiting = True
        self.copy.start()

    def wait(self):
        if self.waiting:
            self.copy.wait()
            self.waiting = False

    def __getitem__(self, index):
        self.wait()
        return self.target[index]


class Stages:
    def __init__(self, groups, depth):
        self.groups, self.depth = groups, depth
        for copy in sum(groups[:depth], []):
            copy.start()

    def wait(self, n):
        for copy in self.groups[n]:
            copy.wait()
        for copy in sum(self.groups[n + self.depth : n + self.depth + 1], []):
            copy.start()


def call(kernel, name, outs, place, *args, raw=0, direct=0, near=0, scratch=(), limit=28 << 20, far=False):
    count, given = len(outs) - direct, len(args) - raw - near

    def body(place_ref, *refs):
        raw_refs, ins, refs = refs[:raw], refs[raw : raw + given], refs[raw + given :]
        near_refs, refs = refs[:near], refs[near:]
        out_refs, direct_refs, refs = refs[:count], refs[count : count + direct], refs[count + direct :]
        held, made, refs = refs[:given], refs[given : given + count], refs[given + count :]
        in_sems, out_sems, own = refs[0], refs[1], refs[2:]
        loaded = [Loaded(ins[n], held[n], in_sems.at[n]) for n in range(given)]
        kernel(place_ref, *raw_refs, *loaded, *near_refs, *made, *direct_refs, *own)
        for held_ref in loaded:
            held_ref.wait()
        copies = [pltpu.make_async_copy(made[n], out_refs[n], out_sems.at[n]) for n in range(count)]
        for copy in copies:
            copy.start()
        for copy in copies:
            copy.wait()

    return pl.pallas_call(
        body,
        in_specs=[SMEM] + [HBM] * (raw + given) + [VMEM] * near,
        out_specs=[HBM] * len(outs),
        out_shape=[pltpu.HBM(*out) if far else jax.ShapeDtypeStruct(*out) for out in outs],
        scratch_shapes=[pltpu.VMEM(x.shape, x.dtype) for x in args[raw : raw + given]]
        + [pltpu.VMEM(shape, kind) for shape, kind in outs[:count]]
        + [pltpu.SemaphoreType.DMA((max(given, 1),)), pltpu.SemaphoreType.DMA((max(count, 1),)), *scratch],
        compiler_params=pltpu.CompilerParams(vmem_limit_bytes=limit),
        name=name,
    )(place, *args)


def call_near(kernel, name, outs, place, *args, direct=0, scratch=(), limit=28 << 20):
    count = len(outs) - direct
    return pl.pallas_call(
        kernel,
        in_specs=[SMEM] + [VMEM] * len(args),
        out_specs=[VMEM] * count + [HBM] * direct,
        out_shape=[jax.ShapeDtypeStruct(*out) for out in outs[:count]] + [pltpu.HBM(*out) for out in outs[count:]],
        scratch_shapes=list(scratch),
        compiler_params=pltpu.CompilerParams(vmem_limit_bytes=limit),
        name=name,
    )(place, *args)


def column(row):
    n = row.shape[1]
    here = lax.broadcasted_iota(jnp.int32, (n, n), 0) == lax.broadcasted_iota(jnp.int32, (n, n), 1)
    return jnp.sum(jnp.where(here, row, 0.0), axis=1, keepdims=True)


def row(column):
    n = column.shape[0]
    here = lax.broadcasted_iota(jnp.int32, (n, n), 0) == lax.broadcasted_iota(jnp.int32, (n, n), 1)
    return jnp.sum(jnp.where(here, column, 0.0), axis=0, keepdims=True)


def columns(start, size):
    return pl.ds(pl.multiple_of(start, size), size)


def slot_mask(core, ids, lines):
    tokens = ids[0].shape[0]
    own = tokens // CORES
    line = lax.broadcasted_iota(jnp.int32, (tokens, lines), 1)
    expert = (line // (2 * SLOTS)).astype(F32)
    named = [jnp.where(some == expert, 1.0, 0.0) for some in ids]
    total = named[0] + named[1] + named[2] + named[3]
    after = lax.broadcasted_iota(jnp.int32, (tokens, tokens), 0)
    before = lax.broadcasted_iota(jnp.int32, (tokens, tokens), 1)
    earlier = jnp.where((before < after) & (before // own == after // own), 1.0, 0.0)
    rank = dot(earlier.astype(BF16), total.astype(BF16)).astype(jnp.int32)
    token = lax.broadcasted_iota(jnp.int32, (tokens, lines), 0)
    place = rank + ((token // own) ^ core) * CAP
    mask = jnp.where((total > 0.0) & (place == line % SLOTS), 1.0, 0.0)
    return mask, named


def both_of(refs, k):
    return jnp.concatenate([column(ref[k : k + 1, :].astype(F32)) for ref in refs], axis=0)


def build_kernel(place_ref, ids_ref, other_ids_ref, *refs):
    scaled = len(refs) > 5
    if scaled:
        comb_refs, rows_refs, (picks_ref, out_hbm, out_ref, sems) = refs[0:2], refs[2:4], refs[4:]
    else:
        rows_refs, (out_hbm, out_ref, sems) = refs[0:2], refs[2:]
    core = place_ref[0]
    steps, lines, step = out_ref.shape
    tok, width = rows_refs[0].shape
    half = width // CORES
    ids_refs = (ids_ref, other_ids_ref)
    mask, named = slot_mask(core, [both_of(ids_refs, k) for k in range(TOPK)], lines)
    pick = mask.astype(BF16)
    if scaled:
        picks_ref[: CORES * tok, :] = pick
        for k in range(TOPK):
            picks_ref[(k + 1) * CORES * tok : (k + 2) * CORES * tok, :] = (mask * named[k]).astype(BF16)
        chosen = sum(named[k] * both_of(comb_refs, k) for k in range(TOPK)) * mask
        high = chosen.astype(BF16)
        ones = jnp.ones((mask.shape[0], META), BF16)
        weight = dot(high, ones, TN) + dot((chosen - high.astype(F32)).astype(BF16), ones, TN)
        weight = weight[:, :1]
    copies = []
    for n in range(steps):
        cols = columns(core * half + n * step, step)
        found = dot(pick, jnp.concatenate([ref[:, cols] for ref in rows_refs], axis=0), TN)
        out_ref[n] = (found * weight if scaled else found).astype(BF16)
        copies.append(pltpu.make_async_copy(out_ref.at[n], out_hbm.at[:, pl.ds(n * step, step)], sems.at[n]))
        copies[-1].start()
    for copy in copies:
        copy.wait()


def build_rows_kernel(place_ref, ids_ref, rows_ref, other_ids_ref, other_rows_ref, *refs):
    build_kernel(place_ref, ids_ref, other_ids_ref, rows_ref, other_rows_ref, *refs)


def lend_kernel(place_ref, gate_hbm, up_hbm, order_hbm, first_ref, sems):
    half, both = first_ref.shape
    ff = both // 2
    at = columns((1 - place_ref[0]) * half, half)
    copies = [
        pltpu.make_async_copy(gate_hbm.at[0, at, :], first_ref.at[:, pl.ds(0, ff)], sems.at[0]),
        pltpu.make_async_copy(up_hbm.at[0, at, :], first_ref.at[:, pl.ds(ff, ff)], sems.at[1]),
    ]
    for copy in copies:
        copy.start()
    for copy in copies:
        copy.wait()


def turn_kernel(place_ref, gate_ref, up_ref, down_ref, lent_ref, back_ref, own_ref, other_ref):
    half = lent_ref.shape[0]
    ff, width = down_ref.shape[1:]
    step = 256
    for n in range(0, width, step):
        back_ref[n : n + step, :] = down_ref[0, :, n : n + step].T
    for n in range(0, half, step):
        at = columns(place_ref[0] * half + n, step)
        own_ref[:ff, n : n + step] = gate_ref[0, at, :].T
        own_ref[ff:, n : n + step] = up_ref[0, at, :].T
        other_ref[:, n : n + step] = lent_ref[n : n + step, :].T


def gate_up_kernel(place_ref, gate_hbm, up_hbm, own_hbm, other_hbm, factors_ref, hidden_ref, rows_ref, first_ref, sems):
    core = place_ref[0]
    parts, step, both = first_ref.shape
    ff = both // 2
    half = parts * step // CORES
    groups = []
    for n in range(parts):
        j, at = divmod(n * step, half)
        cols = columns((core ^ j) * half + at, step)
        pairs = (
            ((own_hbm, other_hbm)[j].at[:, pl.ds(at, step)], rows_ref.at[n]),
            (gate_hbm.at[0, cols, :], first_ref.at[n, :, pl.ds(0, ff)]),
            (up_hbm.at[0, cols, :], first_ref.at[n, :, pl.ds(ff, ff)]),
        )
        groups.append([pltpu.make_async_copy(*pair, sems.at[3 * n + k]) for k, pair in enumerate(pairs)])
    stages = Stages(groups, 2)
    pre = 0.0
    for n in range(parts):
        stages.wait(n)
        pre += dot(rows_ref[n], first_ref[n])
    gate_pre, up_pre = pre[:, :ff], pre[:, ff:]
    sigmoid_gate = jax.nn.sigmoid(gate_pre)
    active = gate_pre * sigmoid_gate
    hidden_ref[...] = (active * up_pre).astype(BF16)
    factors_ref[:, :ff] = up_pre * sigmoid_gate * (1.0 + gate_pre * (1.0 - sigmoid_gate))
    factors_ref[:, ff:] = active


def back_product(which, back_ref, grads_ref):
    half = grads_ref.shape[1]
    return dot(grads_ref[...], back_ref[columns(which * half, half), :])


def back_early_kernel(place_ref, back_hbm, own_hbm, out_ref, back_ref, own_ref, sems):
    steps, step, _ = back_ref.shape
    half = steps * step
    groups = [
        [
            pltpu.make_async_copy(own_hbm.at[:, pl.ds(n * step, step)], own_ref.at[n], sems.at[2 * n]),
            pltpu.make_async_copy(back_hbm.at[columns(place_ref[0] * half + n * step, step), :], back_ref.at[n], sems.at[2 * n + 1]),
        ]
        for n in range(steps)
    ]
    stages = Stages(groups, steps)
    scaled = 0.0
    for n in range(steps):
        stages.wait(n)
        scaled += dot(own_ref[n], back_ref[n])
    out_ref[...] = scaled


def back_late_kernel(place_ref, back_ref, other_ref, sum_ref, factors_ref, hidden_ref, deltas_ref, score_ref):
    scaled = back_product(1 - place_ref[0], back_ref, other_ref) + sum_ref[...]
    ff = scaled.shape[1]
    score = jnp.sum(scaled * hidden_ref[...].astype(F32), axis=1, keepdims=True)
    deltas_ref[:, :ff] = (scaled * factors_ref[:, :ff]).astype(BF16)
    deltas_ref[:, ff:] = (scaled * factors_ref[:, ff:]).astype(BF16)
    score_ref[...] = jnp.broadcast_to(score, score_ref.shape).astype(BF16)


def parts_own_kernel(place_ref, turned_ref, deltas_ref, out_ref):
    step = 512
    deltas = deltas_ref[...]
    for at in range(0, out_ref.shape[1], step):
        out_ref[:, at : at + step] = dot(deltas, turned_ref[:, at : at + step]).astype(BF16)


def parts_sum_kernel(place_ref, turned_ref, deltas_ref, before_ref, score_ref, out_hbm, part_ref, sems):
    steps, _, step = part_ref.shape
    half = steps * step
    outs = [pltpu.make_async_copy(score_ref, out_hbm.at[:, pl.ds(half, META)], sems.at[steps])]
    outs[0].start()
    deltas = deltas_ref[...]
    for n in range(steps):
        at = n * step
        part = dot(deltas, turned_ref[:, at : at + step]) + before_ref[:, at : at + step].astype(F32)
        part_ref[n] = part.astype(BF16)
        outs.append(pltpu.make_async_copy(part_ref.at[n], out_hbm.at[:, pl.ds(at, step)], sems.at[n]))
        outs[-1].start()
    for copy in outs:
        copy.wait()


def gather_kernel(place_ref, back_ref, picks_ref, mine_ref, send_ref, mine_score_ref, send_score_ref):
    tok, width = mine_ref.shape
    tokens = CORES * tok
    step = 512
    pick = picks_ref[:tokens, :]
    for at in range(0, width, step):
        part = dot(pick, back_ref[:, at : at + step]).astype(BF16)
        mine_ref[:, at : at + step] = part[:tok]
        send_ref[:, at : at + step] = part[tok:]
    scores = dot(picks_ref[tokens:, :], back_ref[:, width:])
    for k in range(TOPK):
        mine_score_ref[k : k + 1, :] = row(scores[k * tokens : k * tokens + tok, :1])
        send_score_ref[k : k + 1, :] = row(scores[k * tokens + tok : (k + 1) * tokens, :1])


def weights_kernel(place_ref, *refs):
    rows_refs, grads_refs = refs[0:2], refs[2:4]
    deltas_ref, hidden_ref, given_ref, picks_ref, gate_hbm, up_hbm, down_hbm, gate_ref, up_ref, down_ref, sems = refs[4:]
    picks_ref[...] = given_ref[...]
    core = place_ref[0]
    half, step = rows_refs[0].shape[1], gate_ref.shape[1]
    ff = hidden_ref.shape[1]
    deltas = deltas_ref[...]
    copies = []
    for j in range(CORES):
        for at in range(0, half, step):
            n = (j * half + at) // step
            grad = dot(rows_refs[j][:, at : at + step], deltas, TN)
            gate_ref[n] = grad[:, :ff].astype(BF16)
            up_ref[n] = grad[:, ff:].astype(BF16)
            cols = columns((core ^ j) * half + at, step)
            copies += [
                pltpu.make_async_copy(gate_ref.at[n], gate_hbm.at[0, cols, :], sems.at[3 * n]),
                pltpu.make_async_copy(up_ref.at[n], up_hbm.at[0, cols, :], sems.at[3 * n + 1]),
            ]
            for copy in copies[-2:]:
                copy.start()
    hidden = hidden_ref[...].T
    for j in range(CORES):
        for at in range(0, half, step):
            n = (j * half + at) // step
            down_ref[n] = dot(hidden, grads_refs[j][:, at : at + step]).astype(BF16)
            cols = columns((core ^ j) * half + at, step)
            copies.append(pltpu.make_async_copy(down_ref.at[n], down_hbm.at[0, :, cols], sems.at[3 * n + 2]))
            copies[-1].start()
    for copy in copies:
        copy.wait()


def local(tokens, out_grad, combine, expert_ids, gate_weight, up_weight, down_weight):
    tok, width = tokens.shape
    chips = lax.axis_size(CHIPS)
    lines = chips * SLOTS
    ff = gate_weight.shape[2]
    half, quarter = width // CORES, width // CORES // 2
    step = 512
    place = lax.axis_index("core").astype(jnp.int32).reshape(1)

    def swap(x):
        return lax.ppermute(x, "core", [(0, 1), (1, 0)])

    def deliver(x):
        found = lax.all_to_all(x.reshape(chips, SLOTS, x.shape[1]), CHIPS, split_axis=0, concat_axis=0, tiled=True)
        return found.reshape(x.shape)

    ids, comb = expert_ids.T, combine.T
    ids_pair = (ids, swap(ids))
    tokens_pair = (tokens, swap(tokens))
    scratch = [pltpu.VMEM((half // step, lines, step), BF16), pltpu.SemaphoreType.DMA((half // step,))]
    out = ((lines, half), BF16)
    rows_out = call(
        build_rows_kernel, "build_rows", [out],
        place, *[pltpu.with_memory_space_constraint(x, pltpu.HBM) for x in (ids, tokens)], ids_pair[1], tokens_pair[1],
        direct=1, near=2, far=True,
        scratch=[pltpu.VMEM((half // 256, lines, 256), BF16), pltpu.SemaphoreType.DMA((half // 256,))],
    )[0]
    later = after(comb, out_grad, rows_out)[:2]
    comb_pair, out_grad_pair = [(x, swap(x)) for x in later]
    picks, grads_out = call(
        build_kernel, "build_grads", [(((TOPK + 1) * CORES * tok, lines), BF16), out],
        place, *ids_pair, *comb_pair, *out_grad_pair, direct=1, scratch=scratch, far=True,
    )
    lend = call(
        lend_kernel, "lend", [((half, 2 * ff), BF16)], place, gate_weight, up_weight, out_grad_pair[1],
        raw=3, scratch=[pltpu.SemaphoreType.DMA((2,))],
    )[0]
    rows, grads_out, lend = after(deliver(rows_out), grads_out, lend)
    back, parts_own, parts_other = call_near(
        turn_kernel,
        "turn",
        [((width, ff), BF16)] + [((2 * ff, half), BF16)] * CORES,
        place, gate_weight, up_weight, down_weight, swap(lend),
    )
    rows_pair = (rows, swap(rows))
    factors, hidden = call(
        gate_up_kernel,
        "gate_up",
        [((lines, 2 * ff), F32), ((lines, ff), BF16)],
        place, gate_weight, up_weight, *rows_pair,
        raw=4,
        scratch=[
            pltpu.VMEM((4, lines, quarter), BF16),
            pltpu.VMEM((4, quarter, 2 * ff), BF16),
            pltpu.SemaphoreType.DMA((12,)),
        ],
    )
    grads, factors, hidden, back, parts_own, parts_other = after(
        deliver(grads_out), factors, hidden, back, parts_own, parts_other
    )
    grads_pair = (grads, swap(grads))
    scaled = call(
        back_early_kernel,
        "back_early",
        [((lines, ff), F32)],
        place, pltpu.with_memory_space_constraint(back, pltpu.HBM), grads,
        raw=2,
        scratch=[
            pltpu.VMEM((CORES, quarter, ff), BF16),
            pltpu.VMEM((CORES, lines, quarter), BF16),
            pltpu.SemaphoreType.DMA((2 * CORES,)),
        ],
    )[0]
    other, scaled = after(grads_pair[1], scaled)
    deltas, score = call_near(
        back_late_kernel,
        "back_late",
        [((lines, 2 * ff), BF16), ((lines, META), BF16)],
        place, back, other, scaled, factors, hidden,
    )
    part = call_near(parts_own_kernel, "parts_own", [((lines, half), BF16)], place, parts_own, deltas)[0]
    deltas_other, part = after(swap(deltas), part)
    parts_sum = call_near(
        parts_sum_kernel,
        "parts_sum",
        [((lines, half + META), BF16)],
        place, parts_other, deltas_other, part, score,
        direct=1,
        scratch=[pltpu.VMEM((half // step, lines, step), BF16), pltpu.SemaphoreType.DMA((half // step + 1,))],
    )[0]
    picks, gate_grad, up_grad, down_grad = call(
        weights_kernel,
        "weight_grads",
        [(picks.shape, BF16), (gate_weight.shape, BF16), (up_weight.shape, BF16), (down_weight.shape, BF16)],
        place, *rows_pair, *grads_pair, deltas, hidden, picks,
        direct=3,
        scratch=[
            pltpu.VMEM((width // step, step, ff), BF16),
            pltpu.VMEM((width // step, step, ff), BF16),
            pltpu.VMEM((width // step, ff, step), BF16),
            pltpu.SemaphoreType.DMA((3 * width // step,)),
        ],
    )
    mine, send, mine_score, send_score = call_near(
        gather_kernel,
        "gather_rows",
        [((tok, half), BF16)] * CORES + [((TOPK, tok), F32)] * CORES,
        place, deliver(parts_sum), picks,
    )
    combine_grad = ((mine_score + swap(send_score)) / comb).T
    other = swap(send)
    token_grad = jnp.where(
        place[0] == 0, jnp.concatenate([mine, other], axis=1), jnp.concatenate([other, mine], axis=1)
    )
    return token_grad, combine_grad, gate_grad, up_grad, down_grad


def solution(mesh):
    outer, inner = mesh.devices.shape
    split = Mesh(mesh.devices.reshape(outer, inner // CORES, CORES), ALL)
    flat, deep = P(ALL, None), P(ALL, None, None)
    return jax.shard_map(
        local,
        mesh=split,
        in_specs=(flat, flat, flat, flat, deep, deep, deep),
        out_specs=(flat, flat, deep, deep, deep),
        check_vma=False,
    )
```

```python
import functools

import jax
import jax.numpy as jnp
from jax import lax
from jax.experimental import pallas as pl
from jax.experimental.pallas import tpu as pltpu
from jax.sharding import Mesh
from jax.sharding import PartitionSpec as P

CORES = 2
TOPK = 4
CAP = 4
SLOTS = CORES * CAP
META = 128
CHIPS = ("outer", "z")
ALL = ("outer", "z", "core")
F32 = jnp.float32
BF16 = jnp.bfloat16
TN = (((0,), (0,)), ((), ()))
NT = (((1,), (1,)), ((), ()))
SMEM = pl.BlockSpec(memory_space=pltpu.SMEM)
HBM = pl.BlockSpec(memory_space=pltpu.HBM)
VMEM = pl.BlockSpec(memory_space=pltpu.VMEM)


def dot(a, b, dims=(((1,), (0,)), ((), ()))):
    return lax.dot_general(a, b, dims, preferred_element_type=F32)


def after(x, *others):
    return lax.optimization_barrier((x, *others))


class Loaded:
    def __init__(self, source, target, semaphore):
        self.copy = pltpu.make_async_copy(source, target, semaphore)
        self.target = target
        self.shape = target.shape
        self.waiting = True
        self.copy.start()

    def wait(self):
        if self.waiting:
            self.copy.wait()
            self.waiting = False

    def __getitem__(self, index):
        self.wait()
        return self.target[index]


class Stages:
    def __init__(self, groups, depth):
        self.groups, self.depth = groups, depth
        for copy in sum(groups[:depth], []):
            copy.start()

    def wait(self, n):
        for copy in self.groups[n]:
            copy.wait()
        for copy in sum(self.groups[n + self.depth : n + self.depth + 1], []):
            copy.start()


def call(kernel, name, outs, place, *args, raw=0, direct=0, near=0, scratch=(), limit=28 << 20, far=False):
    count, given = len(outs) - direct, len(args) - raw - near

    def body(place_ref, *refs):
        raw_refs, ins, refs = refs[:raw], refs[raw : raw + given], refs[raw + given :]
        near_refs, refs = refs[:near], refs[near:]
        out_refs, direct_refs, refs = refs[:count], refs[count : count + direct], refs[count + direct :]
        held, made, refs = refs[:given], refs[given : given + count], refs[given + count :]
        in_sems, out_sems, own = refs[0], refs[1], refs[2:]
        loaded = [Loaded(ins[n], held[n], in_sems.at[n]) for n in range(given)]
        kernel(place_ref, *raw_refs, *loaded, *near_refs, *made, *direct_refs, *own)
        for held_ref in loaded:
            held_ref.wait()
        copies = [pltpu.make_async_copy(made[n], out_refs[n], out_sems.at[n]) for n in range(count)]
        for copy in copies:
            copy.start()
        for copy in copies:
            copy.wait()

    return pl.pallas_call(
        body,
        in_specs=[SMEM] + [HBM] * (raw + given) + [VMEM] * near,
        out_specs=[HBM] * len(outs),
        out_shape=[pltpu.HBM(*out) if far else jax.ShapeDtypeStruct(*out) for out in outs],
        scratch_shapes=[pltpu.VMEM(x.shape, x.dtype) for x in args[raw : raw + given]]
        + [pltpu.VMEM(shape, kind) for shape, kind in outs[:count]]
        + [pltpu.SemaphoreType.DMA((max(given, 1),)), pltpu.SemaphoreType.DMA((max(count, 1),)), *scratch],
        compiler_params=pltpu.CompilerParams(vmem_limit_bytes=limit),
        name=name,
    )(place, *args)


def call_near(kernel, name, outs, place, *args, direct=0, scratch=(), limit=28 << 20):
    count = len(outs) - direct
    return pl.pallas_call(
        kernel,
        in_specs=[SMEM] + [VMEM] * len(args),
        out_specs=[VMEM] * count + [HBM] * direct,
        out_shape=[jax.ShapeDtypeStruct(*out) for out in outs[:count]] + [pltpu.HBM(*out) for out in outs[count:]],
        scratch_shapes=list(scratch),
        compiler_params=pltpu.CompilerParams(vmem_limit_bytes=limit),
        name=name,
    )(place, *args)


def column(row):
    n = row.shape[1]
    here = lax.broadcasted_iota(jnp.int32, (n, n), 0) == lax.broadcasted_iota(jnp.int32, (n, n), 1)
    return jnp.sum(jnp.where(here, row, 0.0), axis=1, keepdims=True)


def row(column):
    n = column.shape[0]
    here = lax.broadcasted_iota(jnp.int32, (n, n), 0) == lax.broadcasted_iota(jnp.int32, (n, n), 1)
    return jnp.sum(jnp.where(here, column, 0.0), axis=0, keepdims=True)


def columns(start, size):
    return pl.ds(pl.multiple_of(start, size), size)


def slot_mask(core, ids, lines):
    tokens = ids[0].shape[0]
    own = tokens // CORES
    line = lax.broadcasted_iota(jnp.int32, (tokens, lines), 1)
    expert = (line // (2 * SLOTS)).astype(F32)
    named = [jnp.where(some == expert, 1.0, 0.0) for some in ids]
    total = named[0] + named[1] + named[2] + named[3]
    after = lax.broadcasted_iota(jnp.int32, (tokens, tokens), 0)
    before = lax.broadcasted_iota(jnp.int32, (tokens, tokens), 1)
    earlier = jnp.where((before < after) & (before // own == after // own), 1.0, 0.0)
    rank = dot(earlier.astype(BF16), total.astype(BF16)).astype(jnp.int32)
    token = lax.broadcasted_iota(jnp.int32, (tokens, lines), 0)
    place = rank + ((token // own) ^ core) * CAP
    mask = jnp.where((total > 0.0) & (place == line % SLOTS), 1.0, 0.0)
    return mask, named


def both_of(refs, k):
    return jnp.concatenate([column(ref[k : k + 1, :].astype(F32)) for ref in refs], axis=0)


def build_kernel(place_ref, ids_ref, other_ids_ref, *refs):
    scaled = len(refs) > 5
    if scaled:
        comb_refs, rows_refs, (picks_ref, out_hbm, out_ref, sems) = refs[0:2], refs[2:4], refs[4:]
    else:
        rows_refs, (out_hbm, out_ref, sems) = refs[0:2], refs[2:]
    core = place_ref[0]
    steps, lines, step = out_ref.shape
    tok, width = rows_refs[0].shape
    half = width // CORES
    ids_refs = (ids_ref, other_ids_ref)
    mask, named = slot_mask(core, [both_of(ids_refs, k) for k in range(TOPK)], lines)
    pick = mask.astype(BF16)
    if scaled:
        picks_ref[: CORES * tok, :] = pick
        for k in range(TOPK):
            picks_ref[(k + 1) * CORES * tok : (k + 2) * CORES * tok, :] = (mask * named[k]).astype(BF16)
        chosen = sum(named[k] * both_of(comb_refs, k) for k in range(TOPK)) * mask
        high = chosen.astype(BF16)
        ones = jnp.ones((mask.shape[0], META), BF16)
        weight = dot(high, ones, TN) + dot((chosen - high.astype(F32)).astype(BF16), ones, TN)
        weight = weight[:, :1]
    copies = []
    for n in range(steps):
        cols = columns(core * half + n * step, step)
        found = dot(pick, jnp.concatenate([ref[:, cols] for ref in rows_refs], axis=0), TN)
        out_ref[n] = (found * weight if scaled else found).astype(BF16)
        copies.append(pltpu.make_async_copy(out_ref.at[n], out_hbm.at[:, pl.ds(n * step, step)], sems.at[n]))
        copies[-1].start()
    for copy in copies:
        copy.wait()


def build_rows_kernel(place_ref, ids_ref, rows_ref, other_ids_ref, other_rows_ref, *refs):
    build_kernel(place_ref, ids_ref, other_ids_ref, rows_ref, other_rows_ref, *refs)


def lend_kernel(place_ref, gate_hbm, up_hbm, order_hbm, first_ref, sems):
    half, both = first_ref.shape
    ff = both // 2
    at = columns((1 - place_ref[0]) * half, half)
    copies = [
        pltpu.make_async_copy(gate_hbm.at[0, at, :], first_ref.at[:, pl.ds(0, ff)], sems.at[0]),
        pltpu.make_async_copy(up_hbm.at[0, at, :], first_ref.at[:, pl.ds(ff, ff)], sems.at[1]),
    ]
    for copy in copies:
        copy.start()
    for copy in copies:
        copy.wait()


def turn_kernel(place_ref, gate_ref, up_ref, down_ref, lent_ref, back_ref, own_ref, other_ref):
    half = lent_ref.shape[0]
    ff, width = down_ref.shape[1:]
    step = 256
    for n in range(0, width, step):
        back_ref[n : n + step, :] = down_ref[0, :, n : n + step].T
    for n in range(0, half, step):
        at = columns(place_ref[0] * half + n, step)
        own_ref[:ff, n : n + step] = gate_ref[0, at, :].T
        own_ref[ff:, n : n + step] = up_ref[0, at, :].T
        other_ref[:, n : n + step] = lent_ref[n : n + step, :].T


def gate_up_kernel(place_ref, gate_hbm, up_hbm, own_hbm, other_hbm, factors_ref, hidden_ref, rows_ref, first_ref, sems):
    core = place_ref[0]
    parts, step, both = first_ref.shape
    ff = both // 2
    half = parts * step // CORES
    groups = []
    for n in range(parts):
        j, at = divmod(n * step, half)
        cols = columns((core ^ j) * half + at, step)
        pairs = (
            ((own_hbm, other_hbm)[j].at[:, pl.ds(at, step)], rows_ref.at[n]),
            (gate_hbm.at[0, cols, :], first_ref.at[n, :, pl.ds(0, ff)]),
            (up_hbm.at[0, cols, :], first_ref.at[n, :, pl.ds(ff, ff)]),
        )
        groups.append([pltpu.make_async_copy(*pair, sems.at[3 * n + k]) for k, pair in enumerate(pairs)])
    stages = Stages(groups, 2)
    pre = 0.0
    for n in range(parts):
        stages.wait(n)
        pre += dot(rows_ref[n], first_ref[n])
    gate_pre, up_pre = pre[:, :ff], pre[:, ff:]
    sigmoid_gate = jax.nn.sigmoid(gate_pre)
    active = gate_pre * sigmoid_gate
    hidden_ref[...] = (active * up_pre).astype(BF16)
    factors_ref[:, :ff] = up_pre * sigmoid_gate * (1.0 + gate_pre * (1.0 - sigmoid_gate))
    factors_ref[:, ff:] = active


def back_product(which, back_ref, grads_ref):
    half = grads_ref.shape[1]
    return dot(grads_ref[...], back_ref[columns(which * half, half), :])


def back_early_kernel(place_ref, back_hbm, own_hbm, out_ref, back_ref, own_ref, sems):
    steps, step, _ = back_ref.shape
    half = steps * step
    groups = [
        [
            pltpu.make_async_copy(own_hbm.at[:, pl.ds(n * step, step)], own_ref.at[n], sems.at[2 * n]),
            pltpu.make_async_copy(back_hbm.at[columns(place_ref[0] * half + n * step, step), :], back_ref.at[n], sems.at[2 * n + 1]),
        ]
        for n in range(steps)
    ]
    stages = Stages(groups, steps)
    scaled = 0.0
    for n in range(steps):
        stages.wait(n)
        scaled += dot(own_ref[n], back_ref[n])
    out_ref[...] = scaled


def back_late_kernel(place_ref, back_ref, other_ref, sum_ref, factors_ref, hidden_ref, deltas_ref, score_ref):
    scaled = back_product(1 - place_ref[0], back_ref, other_ref) + sum_ref[...]
    ff = scaled.shape[1]
    score = jnp.sum(scaled * hidden_ref[...].astype(F32), axis=1, keepdims=True)
    deltas_ref[:, :ff] = (scaled * factors_ref[:, :ff]).astype(BF16)
    deltas_ref[:, ff:] = (scaled * factors_ref[:, ff:]).astype(BF16)
    score_ref[...] = jnp.broadcast_to(score, score_ref.shape).astype(BF16)


def parts_own_kernel(place_ref, turned_ref, deltas_ref, out_ref):
    step = 512
    deltas = deltas_ref[...]
    for at in range(0, out_ref.shape[1], step):
        out_ref[:, at : at + step] = dot(deltas, turned_ref[:, at : at + step]).astype(BF16)


def parts_sum_kernel(place_ref, turned_ref, deltas_ref, before_ref, score_ref, out_hbm, part_ref, sems):
    steps, _, step = part_ref.shape
    half = steps * step
    outs = [pltpu.make_async_copy(score_ref, out_hbm.at[:, pl.ds(half, META)], sems.at[steps])]
    outs[0].start()
    deltas = deltas_ref[...]
    for n in range(steps):
        at = n * step
        part = dot(deltas, turned_ref[:, at : at + step]) + before_ref[:, at : at + step].astype(F32)
        part_ref[n] = part.astype(BF16)
        outs.append(pltpu.make_async_copy(part_ref.at[n], out_hbm.at[:, pl.ds(at, step)], sems.at[n]))
        outs[-1].start()
    for copy in outs:
        copy.wait()


def gather_kernel(place_ref, back_ref, picks_ref, mine_ref, send_ref, mine_score_ref, send_score_ref):
    tok, width = mine_ref.shape
    tokens = CORES * tok
    step = 512
    pick = picks_ref[:tokens, :]
    for at in range(0, width, step):
        part = dot(pick, back_ref[:, at : at + step]).astype(BF16)
        mine_ref[:, at : at + step] = part[:tok]
        send_ref[:, at : at + step] = part[tok:]
    scores = dot(picks_ref[tokens:, :], back_ref[:, width:])
    for k in range(TOPK):
        mine_score_ref[k : k + 1, :] = row(scores[k * tokens : k * tokens + tok, :1])
        send_score_ref[k : k + 1, :] = row(scores[k * tokens + tok : (k + 1) * tokens, :1])


def weights_kernel(place_ref, *refs):
    rows_refs, grads_refs = refs[0:2], refs[2:4]
    deltas_ref, hidden_ref, given_ref, picks_ref, gate_hbm, up_hbm, down_hbm, gate_ref, up_ref, down_ref, sems = refs[4:]
    picks_ref[...] = given_ref[...]
    core = place_ref[0]
    half, step = rows_refs[0].shape[1], gate_ref.shape[1]
    ff = hidden_ref.shape[1]
    deltas = deltas_ref[...]
    copies = []
    for j in range(CORES):
        for at in range(0, half, step):
            n = (j * half + at) // step
            grad = dot(rows_refs[j][:, at : at + step], deltas, TN)
            gate_ref[n] = grad[:, :ff].astype(BF16)
            up_ref[n] = grad[:, ff:].astype(BF16)
            cols = columns((core ^ j) * half + at, step)
            copies += [
                pltpu.make_async_copy(gate_ref.at[n], gate_hbm.at[0, cols, :], sems.at[3 * n]),
                pltpu.make_async_copy(up_ref.at[n], up_hbm.at[0, cols, :], sems.at[3 * n + 1]),
            ]
            for copy in copies[-2:]:
                copy.start()
    hidden = hidden_ref[...].T
    for j in range(CORES):
        for at in range(0, half, step):
            n = (j * half + at) // step
            down_ref[n] = dot(hidden, grads_refs[j][:, at : at + step]).astype(BF16)
            cols = columns((core ^ j) * half + at, step)
            copies.append(pltpu.make_async_copy(down_ref.at[n], down_hbm.at[0, :, cols], sems.at[3 * n + 2]))
            copies[-1].start()
    for copy in copies:
        copy.wait()


def local(tokens, out_grad, combine, expert_ids, gate_weight, up_weight, down_weight):
    tok, width = tokens.shape
    chips = lax.axis_size(CHIPS)
    lines = chips * SLOTS
    ff = gate_weight.shape[2]
    half, quarter = width // CORES, width // CORES // 2
    step = 512
    place = lax.axis_index("core").astype(jnp.int32).reshape(1)

    def swap(x):
        return lax.ppermute(x, "core", [(0, 1), (1, 0)])

    def deliver(x):
        found = lax.all_to_all(x.reshape(chips, SLOTS, x.shape[1]), CHIPS, split_axis=0, concat_axis=0, tiled=True)
        return found.reshape(x.shape)

    ids, comb = expert_ids.T, combine.T
    ids_pair = (ids, swap(ids))
    tokens_pair = (tokens, swap(tokens))
    scratch = [pltpu.VMEM((half // step, lines, step), BF16), pltpu.SemaphoreType.DMA((half // step,))]
    out = ((lines, half), BF16)
    rows_out = call(
        build_rows_kernel, "build_rows", [out],
        place, *[pltpu.with_memory_space_constraint(x, pltpu.HBM) for x in (ids, tokens)], ids_pair[1], tokens_pair[1],
        direct=1, near=2, far=True,
        scratch=[pltpu.VMEM((half // 256, lines, 256), BF16), pltpu.SemaphoreType.DMA((half // 256,))],
    )[0]
    later = after(comb, out_grad, rows_out)[:2]
    comb_pair, out_grad_pair = [(x, swap(x)) for x in later]
    picks, grads_out = call(
        build_kernel, "build_grads", [(((TOPK + 1) * CORES * tok, lines), BF16), out],
        place, *ids_pair, *comb_pair, *out_grad_pair, direct=1, scratch=scratch, far=True,
    )
    lend = call(
        lend_kernel, "lend", [((half, 2 * ff), BF16)], place, gate_weight, up_weight, out_grad_pair[1],
        raw=3, scratch=[pltpu.SemaphoreType.DMA((2,))],
    )[0]
    rows, grads_out, lend = after(deliver(rows_out), grads_out, lend)
    back, parts_own, parts_other = call_near(
        turn_kernel,
        "turn",
        [((width, ff), BF16)] + [((2 * ff, half), BF16)] * CORES,
        place, gate_weight, up_weight, down_weight, swap(lend),
    )
    rows_pair = (rows, swap(rows))
    factors, hidden = call(
        gate_up_kernel,
        "gate_up",
        [((lines, 2 * ff), F32), ((lines, ff), BF16)],
        place, gate_weight, up_weight, *rows_pair,
        raw=4,
        scratch=[
            pltpu.VMEM((4, lines, quarter), BF16),
            pltpu.VMEM((4, quarter, 2 * ff), BF16),
            pltpu.SemaphoreType.DMA((12,)),
        ],
    )
    grads, factors, hidden, back, parts_own, parts_other = after(
        deliver(grads_out), factors, hidden, back, parts_own, parts_other
    )
    grads_pair = (grads, swap(grads))
    scaled = call(
        back_early_kernel,
        "back_early",
        [((lines, ff), F32)],
        place, pltpu.with_memory_space_constraint(back, pltpu.HBM), grads,
        raw=2,
        scratch=[
            pltpu.VMEM((CORES, quarter, ff), BF16),
            pltpu.VMEM((CORES, lines, quarter), BF16),
            pltpu.SemaphoreType.DMA((2 * CORES,)),
        ],
    )[0]
    other, scaled = after(grads_pair[1], scaled)
    deltas, score = call_near(
        back_late_kernel,
        "back_late",
        [((lines, 2 * ff), BF16), ((lines, META), BF16)],
        place, back, other, scaled, factors, hidden,
    )
    part = call_near(parts_own_kernel, "parts_own", [((lines, half), BF16)], place, parts_own, deltas)[0]
    deltas_other, part = after(swap(deltas), part)
    parts_sum = call_near(
        parts_sum_kernel,
        "parts_sum",
        [((lines, half + META), BF16)],
        place, parts_other, deltas_other, part, score,
        direct=1,
        scratch=[pltpu.VMEM((half // quarter, lines, quarter), BF16), pltpu.SemaphoreType.DMA((half // quarter + 1,))],
    )[0]
    picks, gate_grad, up_grad, down_grad = call(
        weights_kernel,
        "weight_grads",
        [(picks.shape, BF16), (gate_weight.shape, BF16), (up_weight.shape, BF16), (down_weight.shape, BF16)],
        place, *rows_pair, *grads_pair, deltas, hidden, picks,
        direct=3,
        scratch=[
            pltpu.VMEM((width // step, step, ff), BF16),
            pltpu.VMEM((width // step, step, ff), BF16),
            pltpu.VMEM((width // step, ff, step), BF16),
            pltpu.SemaphoreType.DMA((3 * width // step,)),
        ],
    )
    mine, send, mine_score, send_score = call_near(
        gather_kernel,
        "gather_rows",
        [((tok, half), BF16)] * CORES + [((TOPK, tok), F32)] * CORES,
        place, deliver(parts_sum), picks,
    )
    combine_grad = ((mine_score + swap(send_score)) / comb).T
    other = swap(send)
    token_grad = jnp.where(
        place[0] == 0, jnp.concatenate([mine, other], axis=1), jnp.concatenate([other, mine], axis=1)
    )
    return token_grad, combine_grad, gate_grad, up_grad, down_grad


def solution(mesh):
    outer, inner = mesh.devices.shape
    split = Mesh(mesh.devices.reshape(outer, inner // CORES, CORES), ALL)
    flat, deep = P(ALL, None), P(ALL, None, None)
    return jax.shard_map(
        local,
        mesh=split,
        in_specs=(flat, flat, flat, flat, deep, deep, deep),
        out_specs=(flat, flat, deep, deep, deep),
        check_vma=False,
    )
```
